32 devices in a mesh: space: 8 (over z, y), chan: 4 (over x, core).
Axes of the slice: x: 2, y: 2, z: 4, core: 2. Of those that a mesh axis runs over, the one named last changes fastest.
Arguments:
- features: bfloat16 [128, 16, 512], P('chan', 'space'), may hold values from -6 to 6
- mask_packed: int32 [16, 16], P('space'), may hold values from -2147483648 to 2147483646
- neighbours: int32 [16, 26], P('space'), may hold values from 0 to 10, as said below
- send_list: int32 [8, 8, 1], P('space'), may hold values from 0 to 2, as said below
- weights: bfloat16 [27, 128, 128], P(None, 'chan'), may hold values from -0.109375 to 0.109375
- cotangent: bfloat16 [128, 16, 512], P('chan', 'space'), may hold values from -6 to 6
Outputs:
- activated: bfloat16 [128, 16, 512], P('chan', 'space')
- grad_features: bfloat16 [128, 16, 512], P('chan', 'space')
- grad_weights: float32 [27, 128, 128], P(None, 'chan')
The draws below stay inside these ranges and needn't reach their ends.
Inputs may be any that keep to these rules, and one draw needn't show every extreme that they name: `neighbours`: entry j of a brick's row names the neighbour at the j-th of the 26 offsets as a row of its partition's table: 0 to 1 the partition's own bricks, 2 + k + s the s-th brick received from the adjacent tile in the k-th planar move, used only where the offset's planar part is that move and the tile exists, 10 none. Every slot that is named is filled in send_list. send_list[q, k, s] is the local index of the s-th brick that partition q sends to the partition whose tile lies at q's tile moved by minus the k-th planar move, or 2 where that slot is empty; a slot is filled exactly when some brick of that partition names it.
All inputs are finite; a program needn't handle non-finite values.
Results may differ from the reference program's by a relative error of at most 0.005.
Values may be sent and summed in bfloat16 or wider, within the bound.
A program may use at most 128 MiB of HBM per device.

```python
import math
import jax
import jax.numpy as jnp
from jax import lax

C = 128
BRICK = 8
BRICK_DEV = 2
SLOTS = 1
VOX = 512
BRICKS = 16
N_SPACE = 8


tile_moves = [(move_a, move_b) for move_a in (-1, 0, 1) for move_b in (-1, 0, 1) if (move_a, move_b) != (0, 0)]


cube_offsets = [(along_x, along_y, along_z) for along_x in (-1, 0, 1) for along_y in (-1, 0, 1) for along_z in (-1, 0, 1) if (along_x, along_y, along_z) != (0, 0, 0)]


def move_of(along_x, along_y):
    if (along_x, along_y) == (0, 0):
        return -1
    return tile_moves.index((along_x, along_y))


def geometry(key):
    key_kind, key_local, key_slot, key_pick = jax.random.split(key, 4)
    grid_shape = (N_SPACE, BRICK_DEV, 26)
    category = jax.random.randint(key_kind, grid_shape, 0, 20)
    local_pick = jax.random.randint(key_local, grid_shape, 0, BRICK_DEV)
    slot_pick = jax.random.randint(key_slot, grid_shape, 0, SLOTS)
    offset_x = jnp.array([entry[0] for entry in cube_offsets], dtype=jnp.int32)
    offset_y = jnp.array([entry[1] for entry in cube_offsets], dtype=jnp.int32)
    offset_move = jnp.array([move_of(entry[0], entry[1]) for entry in cube_offsets], dtype=jnp.int32)
    owners = jnp.arange(N_SPACE, dtype=jnp.int32)[:, None, None]
    tile_rows = N_SPACE // 4
    target_x = owners // 4 + offset_x[None, None, :]
    target_y = owners % 4 + offset_y[None, None, :]
    inside = (target_x >= 0) & (target_x < tile_rows) & (target_y >= 0) & (target_y < 4) & (offset_move[None, None, :] >= 0)
    remote_flag = (category >= 13) & inside
    slot_code = offset_move[None, None, :] * SLOTS + slot_pick
    empty_row = BRICK_DEV + 8 * SLOTS
    local_flag = (category >= 7) & ((category < 13) | (offset_move[None, None, :] < 0))
    neighbour_rows = jnp.where(remote_flag, BRICK_DEV + slot_code, jnp.where(local_flag, local_pick, empty_row))
    matches = (slot_code.reshape(N_SPACE, -1)[:, :, None] == jnp.arange(8 * SLOTS, dtype=jnp.int32)[None, None, :]) & remote_flag.reshape(N_SPACE, -1)[:, :, None]
    filled = jnp.any(matches, axis=1).reshape(N_SPACE, 8, SLOTS)
    move_x = jnp.array([entry[0] for entry in tile_moves], dtype=jnp.int32)
    move_y = jnp.array([entry[1] for entry in tile_moves], dtype=jnp.int32)
    senders = jnp.arange(N_SPACE, dtype=jnp.int32)[:, None]
    receiver_x = senders // 4 - move_x[None, :]
    receiver_y = senders % 4 - move_y[None, :]
    receiver_ok = (receiver_x >= 0) & (receiver_x < tile_rows) & (receiver_y >= 0) & (receiver_y < 4)
    receiver = jnp.clip(receiver_x * 4 + receiver_y, 0, N_SPACE - 1)
    sender_filled = filled[receiver, jnp.arange(8, dtype=jnp.int32)[None, :], :] & receiver_ok[:, :, None]
    chosen = jax.random.randint(key_pick, (N_SPACE, 8, SLOTS), 0, BRICK_DEV)
    send_rows = jnp.where(sender_filled, chosen, BRICK_DEV)
    return (neighbour_rows.reshape(N_SPACE * BRICK_DEV, 26).astype(jnp.int32), send_rows.astype(jnp.int32))


def draw_neighbours(key, part):
    neighbour_rows, send_rows = geometry(key)
    return neighbour_rows


def draw_send_list(key, part):
    neighbour_rows, send_rows = geometry(key)
    return send_rows


def set_ends(values, key, least, largest):
    place = [jax.random.randint(jax.random.fold_in(key, axis), (), 0, length) for axis, length in enumerate(values.shape)]
    longest = values.shape.index(max(values.shape))
    neighbour = place[:longest] + [(place[longest] + 1) % values.shape[longest]] + place[longest + 1:]
    return values.at[tuple(place)].set(least).at[tuple(neighbour)].set(largest)


def shard_levels(own_key, shape, shards, smallest, largest):
    loudness, own = 1.0, jax.random.fold_in(own_key, 6)
    for dim, shards_of in shards:
        draws = jnp.exp(jax.random.uniform(jax.random.fold_in(own, dim), (shards_of,), jnp.float32, smallest / len(shards), largest / len(shards)))
        loudness = loudness * jnp.repeat(draws, shape[dim] // shards_of).reshape([-1 if axis == dim else 1 for axis in range(len(shape))])
    return loudness


def centred(stream_key, dims, width, reach, cuts=(), held_as=jnp.bfloat16):
    gain = shard_levels(stream_key, dims, cuts, -0.22, 0.18) if cuts else 1.0
    values = jax.random.normal(stream_key, dims, jnp.float32) * width * gain
    return jnp.minimum(jnp.maximum(values, -reach), reach).astype(held_as)


def setup_inputs(seed: int = 0) -> dict:
    keys = jax.random.split(jax.random.key(seed), 7)
    return {
        "features": centred(keys[0], (C, BRICKS, VOX), 1.0, 6.0, ((0, 4), (1, 8))),
        "mask_packed": set_ends(jax.random.randint(keys[1], (BRICKS, VOX // 32), -2147483648, 2147483647), jax.random.fold_in(keys[1], 1), -2147483648, 2147483646).astype(jnp.int32),
        "neighbours": draw_neighbours(jax.random.fold_in(keys[6], 71), 0),
        "send_list": draw_send_list(jax.random.fold_in(keys[6], 71), 0),
        "weights": centred(keys[4], (27, C, C), (27 * C) ** -0.5, 0.109375, ((1, 4),)),
        "cotangent": centred(keys[5], (C, BRICKS, VOX), 1.0, 6.0, ((0, 4), (1, 8))),
    }


all_offsets = [(along_x, along_y, along_z) for along_x in (-1, 0, 1) for along_y in (-1, 0, 1) for along_z in (-1, 0, 1)]
tile_moves = [(move_a, move_b) for move_a in (-1, 0, 1) for move_b in (-1, 0, 1) if (move_a, move_b) != (0, 0)]
tile_steps = [move_a * 4 + move_b for move_a, move_b in tile_moves]

def unpack_mask(packed):
    shifts = jnp.arange(32, dtype=jnp.int32)
    bitflags = lax.shift_right_logical(packed[:, :, None], shifts[None, None, :]) & 1
    return bitflags.reshape(packed.shape[0], packed.shape[1] * 32).astype(jnp.float32)

def side_slice(direction, extent):
    if direction == -1:
        return slice(extent - 1, extent)
    if direction == 0:
        return slice(0, extent)
    return slice(0, 1)

def cycle_slice(direction, extent):
    if direction == -1:
        return slice(0, 1)
    if direction == 0:
        return slice(1, extent + 1)
    return slice(extent + 1, extent + 2)

def neighbour_slot(along_x, along_y, along_z):
    linear = (along_x + 1) * 9 + (along_y + 1) * 3 + (along_z + 1)
    return linear if linear < 13 else linear - 1

def window_start(extent):
    padded = extent + 2
    return padded * padded + padded + 1

def flat_length(extent):
    padded = extent + 2
    needed = 2 * (padded * padded + padded + 1) + extent * padded * padded
    return (needed + 127) // 128 * 128

def assemble(source_table, center, indices, extent):
    channels, brick_count = (center.shape[0], center.shape[1])
    planes = []
    for along_x in (-1, 0, 1):
        columns = []
        for along_y in (-1, 0, 1):
            pieces = []
            for along_z in (-1, 0, 1):
                if (along_x, along_y, along_z) == (0, 0, 0):
                    source = center
                else:
                    source = jnp.take(source_table, indices[:, neighbour_slot(along_x, along_y, along_z)], axis=1)
                source = source.reshape(channels, brick_count, extent, extent, extent)
                pieces.append(source[:, :, side_slice(along_x, extent), side_slice(along_y, extent), side_slice(along_z, extent)])
            columns.append(jnp.concatenate(pieces, axis=4))
        planes.append(jnp.concatenate(columns, axis=3))
    padded_cube = jnp.concatenate(planes, axis=2)
    padded_edge = extent + 2
    flattened = padded_cube.reshape(channels, brick_count, padded_edge ** 3)
    return jnp.pad(flattened, ((0, 0), (0, 0), (0, flat_length(extent) - padded_edge ** 3)))

def columns_of(padded_block, extent):
    padded = extent + 2
    anchor = window_start(extent)
    length = extent * padded * padded
    windows = []
    for along_x, along_y, along_z in all_offsets:
        offset_flat = along_x * padded * padded + along_y * padded + along_z
        windows.append(padded_block[:, :, anchor + offset_flat:anchor + offset_flat + length])
    return jnp.stack(windows, axis=0)

def interior(window, extent):
    padded = extent + 2
    leading = window.shape[:-1]
    shaped = window.reshape(leading + (extent, padded, padded))[..., :extent, :extent]
    return shaped.reshape(leading + (extent ** 3,))

def embed_window(values, extent):
    padded = extent + 2
    leading = values.shape[:-1]
    shaped = values.reshape(leading + (extent, extent, extent))
    widths = [(0, 0)] * len(leading) + [(0, 0), (0, padded - extent), (0, padded - extent)]
    return jnp.pad(shaped, widths).reshape(leading + (extent * padded * padded,))

def spread(products, extent, full_length, first_offset):
    padded = extent + 2
    anchor = window_start(extent)
    length = products.shape[-1]
    result = jnp.zeros(products.shape[1:-1] + (full_length,), jnp.float32)
    for position in range(products.shape[0]):
        along_x, along_y, along_z = all_offsets[first_offset + position]
        placed_at = anchor + along_x * padded * padded + along_y * padded + along_z
        result = result + jnp.pad(products[position], ((0, 0), (0, 0), (placed_at, full_length - placed_at - length)))
    return result

def scatter_block(grad_block, indices, table_rows, extent):
    channels, brick_count = (grad_block.shape[0], grad_block.shape[1])
    padded = extent + 2
    padded_cube = grad_block[:, :, :padded ** 3].reshape(channels, brick_count, padded, padded, padded)
    interior_span = slice(1, extent + 1)
    center = padded_cube[:, :, interior_span, interior_span, interior_span].reshape(channels, brick_count, extent ** 3)
    accumulated = jnp.zeros((channels, table_rows, extent, extent, extent), jnp.float32)
    for along_x, along_y, along_z in all_offsets:
        if (along_x, along_y, along_z) == (0, 0, 0):
            continue
        column = neighbour_slot(along_x, along_y, along_z)
        rim_piece = padded_cube[:, :, cycle_slice(along_x, extent), cycle_slice(along_y, extent), cycle_slice(along_z, extent)]
        accumulated = accumulated.at[:, indices[:, column], side_slice(along_x, extent), side_slice(along_y, extent), side_slice(along_z, extent)].add(rim_piece)
    return (center, accumulated.reshape(channels, table_rows, extent ** 3))

def reference(features, mask_packed, neighbours, send_list, weights, cotangent):
    mask_full = unpack_mask(mask_packed)
    masked = features * mask_full[None].astype(jnp.bfloat16)
    source_table = jnp.concatenate([masked, jnp.zeros((C, 1, VOX), jnp.bfloat16)], axis=1)
    empty_row = BRICK_DEV + 8 * SLOTS
    weight_rows = weights.reshape(27 * C, C).astype(jnp.float32)
    grad_scale = 1.0 / math.sqrt(BRICKS * VOX)
    step_values = jnp.array(tile_steps, dtype=jnp.int32)
    move_ids = jnp.arange(8, dtype=jnp.int32)

    def partition(running, part_index):
        grad_weight, grad_total = running
        first_brick = part_index * BRICK_DEV
        local_ids = lax.dynamic_slice_in_dim(neighbours, first_brick, BRICK_DEV, 0)
        slot_index = jnp.maximum(local_ids - BRICK_DEV, 0)
        move_index = jnp.minimum(slot_index // SLOTS, 7)
        slot_number = slot_index % SLOTS
        sender = part_index + step_values[move_index]
        sender_inside = (sender >= 0) & (sender < N_SPACE)
        sender_kept = jnp.clip(sender, 0, N_SPACE - 1).astype(jnp.int32)
        sent_local = send_list[sender_kept, move_index, slot_number]
        remote_ids = jnp.where((sent_local >= BRICK_DEV) | ~sender_inside, BRICKS, sender_kept * BRICK_DEV + sent_local)
        global_ids = jnp.where(local_ids < BRICK_DEV, first_brick + local_ids, jnp.where(local_ids < empty_row, remote_ids, BRICKS)).astype(jnp.int32)
        own_bricks = lax.dynamic_slice_in_dim(masked, first_brick, BRICK_DEV, 1)
        own_mask = lax.dynamic_slice_in_dim(mask_full, first_brick, BRICK_DEV, 0)
        padded_block = assemble(source_table, own_bricks, global_ids, BRICK)
        stacked = columns_of(padded_block, BRICK).reshape(27 * C, BRICK_DEV, -1).astype(jnp.float32)
        conv_out = jnp.einsum('rc,rbt->cbt', weight_rows, stacked)
        pre_act = interior(conv_out, BRICK) * own_mask[None]
        gate_value = jax.nn.sigmoid(pre_act)
        activated = (pre_act * gate_value).astype(jnp.bfloat16)
        grad_out = lax.dynamic_slice_in_dim(cotangent, first_brick, BRICK_DEV, 1).astype(jnp.float32)
        grad_conv = (grad_out * own_mask[None] * gate_value * (1.0 + pre_act * (1.0 - gate_value))).astype(jnp.bfloat16)
        grad_window = embed_window(grad_conv, BRICK).astype(jnp.float32)
        grad_weight = grad_weight + jnp.einsum('rbt,cbt->rc', stacked, grad_window)
        products = jnp.einsum('rc,cbt->rbt', weight_rows, grad_window).reshape(27, C, BRICK_DEV, -1)
        grad_block = spread(products, BRICK, padded_block.shape[2], 0)
        center, accumulated = scatter_block(grad_block, local_ids, empty_row + 1, BRICK)
        local_total = center + accumulated[:, :BRICK_DEV]
        current = lax.dynamic_slice_in_dim(grad_total, first_brick, BRICK_DEV, 1)
        grad_total = lax.dynamic_update_slice_in_dim(grad_total, current + local_total, first_brick, 1)
        slot_values = lax.optimization_barrier(accumulated[:, BRICK_DEV:empty_row].astype(jnp.bfloat16)).astype(jnp.float32)
        owners = part_index + step_values
        owners_inside = (owners >= 0) & (owners < N_SPACE)
        owners_kept = jnp.clip(owners, 0, N_SPACE - 1).astype(jnp.int32)
        sent_lists = send_list[owners_kept, move_ids, :]
        targets = jnp.where((sent_lists >= BRICK_DEV) | ~owners_inside[:, None], BRICKS, owners_kept[:, None] * BRICK_DEV + sent_lists).reshape(-1).astype(jnp.int32)
        grad_total = grad_total.at[:, targets].add(slot_values)
        return ((grad_weight, grad_total), activated)
    starting = (jnp.zeros((27 * C, C), jnp.float32), jnp.zeros((C, BRICKS + 1, VOX), jnp.float32))
    (grad_weight, grad_total), outputs = lax.scan(partition, starting, jnp.arange(N_SPACE, dtype=jnp.int32))
    activated = jnp.transpose(outputs, (1, 0, 2, 3)).reshape(C, BRICKS, VOX)
    grad_features = (grad_total[:, :BRICKS] * mask_full[None]).astype(jnp.bfloat16)
    grad_weights = (grad_weight * grad_scale).reshape(27, C, C)
    return (activated, grad_features, grad_weights)
```

```python
import functools
import math

import jax
import jax.numpy as jnp
from jax import lax
from jax.experimental import pallas as pl
from jax.experimental.pallas import tpu as pltpu
from jax.sharding import PartitionSpec as P

BRICK = 8
VOX = 512
LANES = 128
TILES = VOX // LANES
PLANES = BRICK + 2
MESH = pl.DeviceIdType.MESH

tile_moves = [(a, b) for a in (-1, 0, 1) for b in (-1, 0, 1) if (a, b) != (0, 0)]
tile_steps = [a * 4 + b for a, b in tile_moves]
plane_offsets = [(y, z) for y in (-1, 0, 1) for z in (-1, 0, 1)]


def neighbour_slot(along_x, along_y, along_z):
    linear = (along_x + 1) * 9 + (along_y + 1) * 3 + (along_z + 1)
    return linear if linear < 13 else linear - 1


def tile_of(along_x):
    return TILES - 1 if along_x == -1 else 0


def plan_chunks(rows, groups):
    chunk = -(-rows // groups)
    chunk = -(-chunk // 16) * 16
    return chunk, -(-rows // chunk)


def nt_dot(left, right):
    return lax.dot_general(
        left, right, (((1,), (1,)), ((), ())), preferred_element_type=jnp.float32
    )


def nn_dot(left, right):
    return jnp.dot(left, right, preferred_element_type=jnp.float32)


def kernel(
    groups, parts, width, bricks, scale,
    packed, near, sends, feat, w, cot,
    act, grad_feat, grad_w,
    table, outbox, place, expand, w_turned, w_wide, padded, stacked, comp, sum_in, gates,
    window, prod, backbox, back_in, gw_own, gw_send, gw_in, gw_all,
    halo_s, halo_r, back_s, back_r, sum_s, sum_r, gate_s, gate_r, red_s, red_r, all_s, all_r,
):
    me, mine = lax.axis_index("space"), lax.axis_index("chan")
    total = parts * width
    rows_w = 27 * width
    chunk, owners = plan_chunks(rows_w, groups)
    wide = BRICK * LANES
    cube = PLANES * LANES
    f32, bf16 = jnp.float32, jnp.bfloat16

    barrier = pltpu.get_barrier_semaphore()
    for d in range(1, groups):
        pl.semaphore_signal(
            barrier, inc=1, device_id=(lax.rem(me + d, groups), mine), device_id_type=MESH
        )
    for e in range(1, parts):
        pl.semaphore_signal(
            barrier, inc=1, device_id=(me, lax.rem(mine + e, parts)), device_id_type=MESH
        )

    lane = lax.broadcasted_iota(jnp.int32, (1, VOX), 1)
    masks = []
    for b in range(bricks):
        word = jnp.zeros((1, VOX), jnp.int32)
        for i in range(VOX // 32):
            word = jnp.where((lane >> 5) == i, packed[b, i], word)
        masks.append((lax.shift_right_logical(word, lane & 31) & 1).astype(f32))

    masked = [
        feat[:, b * VOX : (b + 1) * VOX].astype(f32) * masks[b] for b in range(bricks)
    ]
    for b in range(bricks):
        for t in range(TILES):
            table[b, t] = masked[b][:, t * LANES : (t + 1) * LANES].astype(bf16)
    table[bricks + 8] = jnp.zeros((TILES, width, LANES), bf16)
    for k, (a, _) in enumerate(tile_moves):
        chosen = jnp.full((width, LANES), sends[0, k, 0], jnp.int32)
        for t in range(TILES) if a == 0 else (tile_of(a),):
            value = jnp.zeros((width, LANES), f32)
            for b in range(bricks):
                value = jnp.where(chosen == b, masked[b][:, t * LANES : (t + 1) * LANES], value)
            outbox[k, t] = value.astype(bf16)

    pl.semaphore_wait(barrier, groups - 1 + parts - 1)

    tile_a, tile_b = me // 4, lax.rem(me, 4)

    def inside(a, b):
        return (
            (tile_a + a >= 0) & (tile_a + a < groups // 4) & (tile_b + b >= 0) & (tile_b + b < 4)
        )

    def halo(k, box, rows, base, send, recv, sign):
        a, _ = tile_moves[k]
        if a == 0:
            source, target = box.at[k], rows.at[base + k]
        else:
            source, target = box.at[k, tile_of(a)], rows.at[base + k, tile_of(a)]
        peer = jnp.clip(me + sign * tile_steps[k], 0, groups - 1)
        return pltpu.make_async_remote_copy(
            src_ref=source, dst_ref=target, send_sem=send.at[k], recv_sem=recv.at[k],
            device_id=(peer, mine), device_id_type=MESH,
        )

    forth = [halo(k, outbox, table, bricks, halo_s, halo_r, -1) for k in range(8)]
    back = [halo(k, backbox, back_in, 0, back_s, back_r, 1) for k in range(8)]
    ahead = [inside(a, b) for a, b in tile_moves]
    behind = [inside(-a, -b) for a, b in tile_moves]

    def start_if(flag, copy):
        @pl.when(flag)
        def _():
            copy.start()

    def sent_if(flag, copy):
        @pl.when(flag)
        def _():
            copy.wait_send()

    def arrived_if(flag, copy):
        @pl.when(flag)
        def _():
            copy.wait_recv()

    for k in range(8):
        start_if(behind[k], forth[k])

    row = lax.broadcasted_iota(jnp.int32, (LANES, 2 * LANES), 0)
    col = lax.broadcasted_iota(jnp.int32, (LANES, 2 * LANES), 1)
    half, at_y, at_z = row >> 6, (row >> 3) & 7, row & 7
    goal = half * LANES + (at_y + 1) * PLANES + (at_z + 1)
    side_y = {-1: at_y == BRICK - 1, 1: at_y == 0}
    side_z = {-1: at_z == BRICK - 1, 1: at_z == 0}
    for n, (y, z) in enumerate(plane_offsets):
        hit = col == goal + (BRICK * PLANES * y + BRICK * z)
        if y != 0:
            hit = hit & side_y[y]
        if z != 0:
            hit = hit & side_z[z]
        place[n] = jnp.where(hit, 1.0, 0.0).astype(bf16)
    expand[...] = jnp.where(col == goal - (PLANES + 1), 1.0, 0.0).astype(bf16)

    rows_k = w_turned.shape[1]
    for c in range(rows_k // LANES):
        have = min(rows_w - c * LANES, LANES)
        block = w[c * LANES : c * LANES + have, :].astype(f32)
        if have < LANES:
            block = jnp.concatenate([block, jnp.zeros((LANES - have, total), f32)], axis=0)
        w_turned[:, c * LANES : (c + 1) * LANES] = block.T.astype(bf16)
    for n in range(9):
        for u in range(3):
            w_wide[n * width : (n + 1) * width, u * total : (u + 1) * total] = w[
                (u * 9 + n) * width : (u * 9 + n + 1) * width, :
            ]
    if rows_k > rows_w:
        stacked[rows_w:, :] = jnp.zeros((rows_k - rows_w, bricks * wide), bf16)
    for u in range(3):
        for b in range(bricks):
            for px in range(PLANES):
                if not u <= px < u + BRICK:
                    window[
                        u * total : (u + 1) * total,
                        b * cube + px * LANES : b * cube + (px + 1) * LANES,
                    ] = jnp.zeros((total, LANES), bf16)

    for k in range(8):
        arrived_if(ahead[k], forth[k])

    built = jnp.zeros((bricks * (TILES + 2) * width, 2 * LANES), f32)
    for n, (y, z) in enumerate(plane_offsets):
        pieces = []
        for b in range(bricks):
            source = b if (y, z) == (0, 0) else near[b, neighbour_slot(0, y, z)]
            pieces.append(table[source].reshape(TILES * width, LANES))
        for x in (-1, 1):
            for b in range(bricks):
                pieces.append(table[near[b, neighbour_slot(x, y, z)], tile_of(x)])
        built = built + nn_dot(jnp.concatenate(pieces, axis=0), place[n])
    ends = bricks * TILES * width
    for b in range(bricks):
        base = b * cube
        low = ends + b * width
        high = ends + (bricks + b) * width
        padded[:, base : base + LANES] = built[low : low + width, LANES:]
        padded[:, base + cube - LANES : base + cube] = built[high : high + width, :LANES]
        for t in range(TILES):
            at = (b * TILES + t) * width
            padded[:, base + (2 * t + 1) * LANES : base + (2 * t + 3) * LANES] = built[
                at : at + width, :
            ]

    length = bricks * cube
    shifts = [(y + 1) * PLANES + (z + 1) for y, z in plane_offsets]
    for n in range(9):
        value = padded[...]
        if shifts[n]:
            value = pltpu.roll(value, length - shifts[n], axis=1)
        value = value.astype(bf16)
        for u in range(3):
            for b in range(bricks):
                stacked[
                    (u * 9 + n) * width : (u * 9 + n + 1) * width, b * wide : (b + 1) * wide
                ] = value[:, b * cube + u * LANES : b * cube + u * LANES + wide]

    def to_owner(b, e):
        peer = lax.rem(mine + e, parts)
        return pltpu.make_async_remote_copy(
            src_ref=comp.at[pl.ds(pl.multiple_of(peer * width, width), width), pl.ds(b * VOX, VOX)],
            dst_ref=sum_in.at[e, :, pl.ds(b * VOX, VOX)],
            send_sem=sum_s.at[b, e], recv_sem=sum_r.at[b, e],
            device_id=(me, peer), device_id_type=MESH,
        )

    own_rows = pl.ds(pl.multiple_of(mine * width, width), width)

    def to_all(b, e):
        peer = lax.rem(mine + e, parts)
        place_at = gates.at[own_rows, pl.ds(b * VOX, VOX)]
        return pltpu.make_async_remote_copy(
            src_ref=place_at, dst_ref=place_at,
            send_sem=gate_s.at[b, e], recv_sem=gate_r.at[b, e],
            device_id=(me, peer), device_id_type=MESH,
        )

    for b in range(bricks):
        for t in range(TILES):
            i = b * TILES + t
            part = nn_dot(w_turned[...], stacked[:, 2 * i * LANES : 2 * (i + 1) * LANES])
            comp[:, i * LANES : (i + 1) * LANES] = nt_dot(
                part.astype(bf16), expand[...]
            ).astype(bf16)
        for e in range(1, parts):
            to_owner(b, e).start()

    for b in range(bricks):
        span = slice(b * VOX, (b + 1) * VOX)
        pre = comp[own_rows, span].astype(f32)
        for e in range(1, parts):
            to_owner(b, e).wait_recv()
            pre = pre + sum_in[e, :, span].astype(f32)
        pre = pre * masks[b]
        gate = jax.nn.sigmoid(pre)
        act[:, span] = (pre * gate).astype(bf16)
        gates[own_rows, span] = (
            cot[:, span].astype(f32) * masks[b] * gate * (1.0 + pre * (1.0 - gate))
        ).astype(bf16)
        for e in range(1, parts):
            to_all(b, e).start()

    for b in range(bricks):
        for e in range(1, parts):
            to_all(b, e).wait_recv()
        for t in range(TILES):
            i = b * TILES + t
            value = nn_dot(gates[:, i * LANES : (i + 1) * LANES], expand[...]).astype(bf16)
            for u in range(3):
                at = b * cube + (u + 2 * t) * LANES
                window[u * total : (u + 1) * total, at : at + 2 * LANES] = value

    reach = owners * chunk
    for start in range(0, reach, reach // 2):
        value = None
        for b in range(bricks):
            term = nt_dot(
                stacked[start : start + reach // 2, b * wide : (b + 1) * wide],
                window[total : 2 * total, b * cube + LANES : b * cube + LANES + wide],
            )
            value = term if value is None else value + term
        gw_own[start : start + reach // 2, :] = value
        gw_send[start : start + reach // 2, :] = value.astype(bf16)

    def chunk_rows(index):
        return pl.ds(pl.multiple_of(index * chunk, 16), chunk)

    def reduce_copy(d):
        peer = lax.rem(me + d, groups)
        kept = jnp.minimum(peer, owners - 1)
        return peer, pltpu.make_async_remote_copy(
            src_ref=gw_send.at[chunk_rows(kept)], dst_ref=gw_in.at[d],
            send_sem=red_s.at[d], recv_sem=red_r.at[d],
            device_id=(peer, mine), device_id_type=MESH,
        )

    kept_me = jnp.minimum(me, owners - 1)

    def share_copy(d):
        peer = lax.rem(me + d, groups)
        span = gw_all.at[chunk_rows(kept_me)]
        return pltpu.make_async_remote_copy(
            src_ref=span, dst_ref=span, send_sem=all_s.at[d], recv_sem=all_r.at[d],
            device_id=(peer, mine), device_id_type=MESH,
        )

    def guarded(flag, action):
        if owners == groups:
            action()
        else:
            pl.when(flag)(action)

    for d in range(1, groups):
        peer, copy = reduce_copy(d)
        guarded(peer < owners, copy.start)

    for i in range(length // (2 * LANES)):
        span = slice(2 * i * LANES, 2 * (i + 1) * LANES)
        prod[:, span] = nn_dot(w_wide[...], window[:, span])
    spread = prod[0:width, :]
    for n in range(1, 9):
        spread = spread + pltpu.roll(prod[n * width : (n + 1) * width, :], shifts[n], axis=1)
    padded[...] = spread

    pieces = []
    blank = jnp.zeros((width, LANES), f32)
    for b in range(bricks):
        for t in range(TILES):
            at = b * cube + (2 * t + 1) * LANES
            pieces.append(padded[:, at : at + 2 * LANES])
    for b in range(bricks):
        pieces.append(jnp.concatenate([blank, padded[:, b * cube : b * cube + LANES]], axis=1))
    for b in range(bricks):
        at = (b + 1) * cube - LANES
        pieces.append(jnp.concatenate([padded[:, at : at + LANES], blank], axis=1))
    rims = jnp.concatenate(pieces, axis=0).astype(bf16)

    whole = TILES * width
    own = [jnp.zeros((whole, LANES), f32) for _ in range(bricks)]
    own_end = {(b, x): blank for b in range(bricks) for x in (-1, 1)}
    slots = [jnp.zeros((whole if a == 0 else width, LANES), f32) for a, _ in tile_moves]

    def picked(index, wanted, value):
        return jnp.where(jnp.full(value.shape, index, jnp.int32) == wanted, value, 0.0)

    for n, (y, z) in enumerate(plane_offsets):
        folded = nt_dot(rims, place[n])
        for x in (-1, 0, 1):
            slot = None if (x, y) == (0, 0) else tile_moves.index((x, y))
            for b in range(bricks):
                if x == 0:
                    piece = folded[b * whole : (b + 1) * whole]
                else:
                    at = ends + (b if x == -1 else bricks + b) * width
                    piece = folded[at : at + width]
                if (x, y, z) == (0, 0, 0):
                    own[b] = own[b] + piece
                    continue
                index = near[b, neighbour_slot(x, y, z)]
                for c in range(bricks):
                    term = picked(index, c, piece)
                    if x == 0:
                        own[c] = own[c] + term
                    else:
                        own_end[c, x] = own_end[c, x] + term
                if slot is not None:
                    slots[slot] = slots[slot] + picked(index, bricks + slot, piece)
    for k, (a, _) in enumerate(tile_moves):
        if a == 0:
            backbox[k] = slots[k].astype(bf16).reshape(TILES, width, LANES)
        else:
            backbox[k, tile_of(a)] = slots[k].astype(bf16)
        start_if(ahead[k], back[k])

    def add_up():
        value = gw_own[chunk_rows(kept_me), :]
        for d in range(1, groups):
            reduce_copy(d)[1].wait_recv()
            value = value + gw_in[d].astype(f32)
        gw_all[chunk_rows(kept_me), :] = (value * scale).astype(bf16)
        for d in range(1, groups):
            share_copy(d).start()

    guarded(me < owners, add_up)

    for k in range(8):
        arrived_if(behind[k], back[k])
    for b in range(bricks):
        for t in range(TILES):
            value = own[b][t * width : (t + 1) * width]
            for x in (-1, 1):
                if t == tile_of(x):
                    value = value + own_end[b, x]
            for k, (a, _) in enumerate(tile_moves):
                if a == 0 or t == tile_of(a):
                    value = value + picked(sends[0, k, 0], b, back_in[k, t].astype(f32))
            at = b * VOX + t * LANES
            grad_feat[:, at : at + LANES] = (
                value * masks[b][:, t * LANES : (t + 1) * LANES]
            ).astype(bf16)

    for d in range(1, groups):
        source = lax.rem(me + groups - d, groups)
        guarded(source < owners, share_copy(d).wait_recv)
    grad_w[...] = gw_all[0:rows_w, :].astype(f32)

    for k in range(8):
        sent_if(behind[k], forth[k])
        sent_if(ahead[k], back[k])
    for b in range(bricks):
        for e in range(1, parts):
            to_owner(b, e).wait_send()
            to_all(b, e).wait_send()
    for d in range(1, groups):
        peer, copy = reduce_copy(d)
        guarded(peer < owners, copy.wait_send)
        guarded(me < owners, share_copy(d).wait_send)


def on_device(features, mask_packed, neighbours, send_list, weights, cotangent):
    groups, parts = lax.axis_size("space"), lax.axis_size("chan")
    width, bricks = features.shape[0], features.shape[1]
    total = weights.shape[2]
    rows_w = 27 * width
    chunk, owners = plan_chunks(rows_w, groups)
    rows_k = -(-max(rows_w, owners * chunk) // LANES) * LANES
    wide, cube = BRICK * LANES, PLANES * LANES
    scale = 1.0 / math.sqrt(bricks * groups * VOX)
    f32, bf16 = jnp.float32, jnp.bfloat16
    vmem = pl.BlockSpec(memory_space=pltpu.VMEM)
    smem = pl.BlockSpec(memory_space=pltpu.SMEM)
    dma = pltpu.SemaphoreType.DMA
    act, grad_feat, grad_w = pl.pallas_call(
        functools.partial(kernel, groups, parts, width, bricks, scale),
        out_shape=(
            jax.ShapeDtypeStruct((width, bricks * VOX), bf16),
            jax.ShapeDtypeStruct((width, bricks * VOX), bf16),
            jax.ShapeDtypeStruct((rows_w, total), f32),
        ),
        in_specs=[smem, smem, smem, vmem, vmem, vmem],
        out_specs=(vmem, vmem, vmem),
        scratch_shapes=[
            pltpu.VMEM((bricks + 9, TILES, width, LANES), bf16),
            pltpu.VMEM((8, TILES, width, LANES), bf16),
            pltpu.VMEM((9, LANES, 2 * LANES), bf16),
            pltpu.VMEM((LANES, 2 * LANES), bf16),
            pltpu.VMEM((total, rows_k), bf16),
            pltpu.VMEM((9 * width, 3 * total), bf16),
            pltpu.VMEM((width, bricks * cube), f32),
            pltpu.VMEM((rows_k, bricks * wide), bf16),
            pltpu.VMEM((total, bricks * VOX), bf16),
            pltpu.VMEM((parts, width, bricks * VOX), bf16),
            pltpu.VMEM((total, bricks * VOX), bf16),
            pltpu.VMEM((3 * total, bricks * cube), bf16),
            pltpu.VMEM((9 * width, bricks * cube), f32),
            pltpu.VMEM((8, TILES, width, LANES), bf16),
            pltpu.VMEM((8, TILES, width, LANES), bf16),
            pltpu.VMEM((owners * chunk, total), f32),
            pltpu.VMEM((owners * chunk, total), bf16),
            pltpu.VMEM((groups, chunk, total), bf16),
            pltpu.VMEM((owners * chunk, total), bf16),
            dma((8,)), dma((8,)), dma((8,)), dma((8,)),
            dma((bricks, parts)), dma((bricks, parts)), dma((bricks, parts)), dma((bricks, parts)),
            dma((groups,)), dma((groups,)), dma((groups,)), dma((groups,)),
        ],
        compiler_params=pltpu.CompilerParams(
            collective_id=0, has_side_effects=True, vmem_limit_bytes=40 * 2**20
        ),
    )(
        mask_packed, neighbours, send_list,
        features.reshape(width, bricks * VOX), weights.reshape(rows_w, total),
        cotangent.reshape(width, bricks * VOX),
    )
    shape = (width, bricks, VOX)
    return act.reshape(shape), grad_feat.reshape(shape), grad_w.reshape(27, width, total)


def solution(mesh):
    return jax.shard_map(
        on_device,
        mesh=mesh,
        in_specs=(
            P("chan", "space", None),
            P("space", None),
            P("space", None),
            P("space", None, None),
            P(None, "chan", None),
            P("chan", "space", None),
        ),
        out_specs=(P("chan", "space", None), P("chan", "space", None), P(None, "chan", None)),
        check_vma=False,
    )
```

```python
import functools
import math

import jax
import jax.numpy as jnp
from jax import lax
from jax.experimental import pallas as pl
from jax.experimental.pallas import tpu as pltpu
from jax.sharding import PartitionSpec as P

BRICK = 8
VOX = 512
LANES = 128
TILES = VOX // LANES
PLANES = BRICK + 2
MESH = pl.DeviceIdType.MESH

tile_moves = [(a, b) for a in (-1, 0, 1) for b in (-1, 0, 1) if (a, b) != (0, 0)]
tile_steps = [a * 4 + b for a, b in tile_moves]
plane_offsets = [(y, z) for y in (-1, 0, 1) for z in (-1, 0, 1)]


def neighbour_slot(along_x, along_y, along_z):
    linear = (along_x + 1) * 9 + (along_y + 1) * 3 + (along_z + 1)
    return linear if linear < 13 else linear - 1


def tile_of(along_x):
    return TILES - 1 if along_x == -1 else 0


def plan_chunks(rows, groups):
    chunk = -(-rows // groups)
    chunk = -(-chunk // 16) * 16
    return chunk, -(-rows // chunk)


def nt_dot(left, right):
    return lax.dot_general(
        left, right, (((1,), (1,)), ((), ())), preferred_element_type=jnp.float32
    )


def nn_dot(left, right):
    return jnp.dot(left, right, preferred_element_type=jnp.float32)


def kernel(
    groups, parts, width, bricks, scale,
    packed, near, sends, feat, w, cot,
    act, grad_feat, grad_w,
    table, outbox, place, expand, w_turned, w_wide, padded, stacked, comp, sum_in, gates,
    window, prod, backbox, back_in, gw_own, gw_send, gw_in, gw_all,
    halo_s, halo_r, back_s, back_r, sum_s, sum_r, gate_s, gate_r, red_s, red_r, all_s, all_r,
):
    me, mine = lax.axis_index("space"), lax.axis_index("chan")
    total = parts * width
    rows_w = 27 * width
    chunk, owners = plan_chunks(rows_w, groups)
    wide = BRICK * LANES
    cube = PLANES * LANES
    f32, bf16 = jnp.float32, jnp.bfloat16

    barrier = pltpu.get_barrier_semaphore()
    for d in range(1, groups):
        pl.semaphore_signal(
            barrier, inc=1, device_id=(lax.rem(me + d, groups), mine), device_id_type=MESH
        )
    for e in range(1, parts):
        pl.semaphore_signal(
            barrier, inc=1, device_id=(me, lax.rem(mine + e, parts)), device_id_type=MESH
        )

    lane = lax.broadcasted_iota(jnp.int32, (1, VOX), 1)
    masks = []
    for b in range(bricks):
        word = jnp.zeros((1, VOX), jnp.int32)
        for i in range(VOX // 32):
            word = jnp.where((lane >> 5) == i, packed[b, i], word)
        masks.append((lax.shift_right_logical(word, lane & 31) & 1).astype(f32))

    masked = [
        feat[:, b, :].astype(f32) * masks[b] for b in range(bricks)
    ]
    for b in range(bricks):
        for t in range(TILES):
            table[b, t] = masked[b][:, t * LANES : (t + 1) * LANES].astype(bf16)
    table[bricks + 8] = jnp.zeros((TILES, width, LANES), bf16)
    for k, (a, _) in enumerate(tile_moves):
        chosen = jnp.full((width, LANES), sends[0, k], jnp.int32)
        for t in range(TILES) if a == 0 else (tile_of(a),):
            value = jnp.zeros((width, LANES), f32)
            for b in range(bricks):
                value = jnp.where(chosen == b, masked[b][:, t * LANES : (t + 1) * LANES], value)
            outbox[k, t] = value.astype(bf16)

    pl.semaphore_wait(barrier, groups - 1 + parts - 1)

    tile_a, tile_b = me // 4, lax.rem(me, 4)

    def inside(a, b):
        return (
            (tile_a + a >= 0) & (tile_a + a < groups // 4) & (tile_b + b >= 0) & (tile_b + b < 4)
        )

    def halo(k, box, rows, base, send, recv, sign):
        a, _ = tile_moves[k]
        if a == 0:
            source, target = box.at[k], rows.at[base + k]
        else:
            source, target = box.at[k, tile_of(a)], rows.at[base + k, tile_of(a)]
        peer = jnp.clip(me + sign * tile_steps[k], 0, groups - 1)
        return pltpu.make_async_remote_copy(
            src_ref=source, dst_ref=target, send_sem=send.at[k], recv_sem=recv.at[k],
            device_id=(peer, mine), device_id_type=MESH,
        )

    forth = [halo(k, outbox, table, bricks, halo_s, halo_r, -1) for k in range(8)]
    back = [halo(k, backbox, back_in, 0, back_s, back_r, 1) for k in range(8)]
    ahead = [inside(a, b) for a, b in tile_moves]
    behind = [inside(-a, -b) for a, b in tile_moves]

    def start_if(flag, copy):
        @pl.when(flag)
        def _():
            copy.start()

    def sent_if(flag, copy):
        @pl.when(flag)
        def _():
            copy.wait_send()

    def arrived_if(flag, copy):
        @pl.when(flag)
        def _():
            copy.wait_recv()

    for k in range(8):
        start_if(behind[k], forth[k])

    row = lax.broadcasted_iota(jnp.int32, (LANES, 2 * LANES), 0)
    col = lax.broadcasted_iota(jnp.int32, (LANES, 2 * LANES), 1)
    half, at_y, at_z = row >> 6, (row >> 3) & 7, row & 7
    goal = half * LANES + (at_y + 1) * PLANES + (at_z + 1)
    side_y = {-1: at_y == BRICK - 1, 1: at_y == 0}
    side_z = {-1: at_z == BRICK - 1, 1: at_z == 0}
    for n, (y, z) in enumerate(plane_offsets):
        hit = col == goal + (BRICK * PLANES * y + BRICK * z)
        if y != 0:
            hit = hit & side_y[y]
        if z != 0:
            hit = hit & side_z[z]
        place[n * LANES : (n + 1) * LANES, :] = jnp.where(hit, 1.0, 0.0).astype(bf16)
    expand[...] = jnp.where(col == goal - (PLANES + 1), 1.0, 0.0).astype(bf16)

    rows_k = w_turned.shape[1]
    for c in range(rows_k // LANES):
        have = min(rows_w - c * LANES, LANES)
        block = w[c * LANES : c * LANES + have, :].astype(f32)
        if have < LANES:
            block = jnp.concatenate([block, jnp.zeros((LANES - have, total), f32)], axis=0)
        w_turned[:, c * LANES : (c + 1) * LANES] = block.T.astype(bf16)
    for n in range(9):
        for u in range(3):
            w_wide[n * width : (n + 1) * width, u * total : (u + 1) * total] = w[
                (u * 9 + n) * width : (u * 9 + n + 1) * width, :
            ]
    if rows_k > rows_w:
        stacked[rows_w:, :] = jnp.zeros((rows_k - rows_w, bricks * wide), bf16)
    for u in range(3):
        for b in range(bricks):
            for px in range(PLANES):
                if not u <= px < u + BRICK:
                    window[
                        u * total : (u + 1) * total,
                        b * cube + px * LANES : b * cube + (px + 1) * LANES,
                    ] = jnp.zeros((total, LANES), bf16)

    for k in range(8):
        arrived_if(ahead[k], forth[k])

    columns = []
    for n, (y, z) in enumerate(plane_offsets):
        pieces = []
        for b in range(bricks):
            source = b if (y, z) == (0, 0) else near[b, neighbour_slot(0, y, z)]
            pieces.append(table[source].reshape(TILES * width, LANES))
        for x in (-1, 1):
            for b in range(bricks):
                pieces.append(table[near[b, neighbour_slot(x, y, z)], tile_of(x)])
        columns.append(jnp.concatenate(pieces, axis=0))
    built = nn_dot(jnp.concatenate(columns, axis=1), place[...])
    ends = bricks * TILES * width
    for b in range(bricks):
        base = b * cube
        low = ends + b * width
        high = ends + (bricks + b) * width
        padded[:, base : base + LANES] = built[low : low + width, LANES:]
        padded[:, base + cube - LANES : base + cube] = built[high : high + width, :LANES]
        for t in range(TILES):
            at = (b * TILES + t) * width
            padded[:, base + (2 * t + 1) * LANES : base + (2 * t + 3) * LANES] = built[
                at : at + width, :
            ]

    length = bricks * cube
    shifts = [(y + 1) * PLANES + (z + 1) for y, z in plane_offsets]
    for n in range(9):
        value = padded[...]
        if shifts[n]:
            value = pltpu.roll(value, length - shifts[n], axis=1)
        value = value.astype(bf16)
        for u in range(3):
            for b in range(bricks):
                stacked[
                    (u * 9 + n) * width : (u * 9 + n + 1) * width, b * wide : (b + 1) * wide
                ] = value[:, b * cube + u * LANES : b * cube + u * LANES + wide]

    def to_owner(b, e):
        peer = lax.rem(mine + e, parts)
        return pltpu.make_async_remote_copy(
            src_ref=comp.at[pl.ds(pl.multiple_of(peer * width, width), width), pl.ds(b * VOX, VOX)],
            dst_ref=sum_in.at[e, :, pl.ds(b * VOX, VOX)],
            send_sem=sum_s.at[b, e], recv_sem=sum_r.at[b, e],
            device_id=(me, peer), device_id_type=MESH,
        )

    own_rows = pl.ds(pl.multiple_of(mine * width, width), width)

    def to_all(b, e):
        peer = lax.rem(mine + e, parts)
        place_at = gates.at[own_rows, pl.ds(b * VOX, VOX)]
        return pltpu.make_async_remote_copy(
            src_ref=place_at, dst_ref=place_at,
            send_sem=gate_s.at[b, e], recv_sem=gate_r.at[b, e],
            device_id=(me, peer), device_id_type=MESH,
        )

    for b in range(bricks):
        for t in range(TILES):
            i = b * TILES + t
            part = nn_dot(w_turned[...], stacked[:, 2 * i * LANES : 2 * (i + 1) * LANES])
            comp[:, i * LANES : (i + 1) * LANES] = nt_dot(
                part.astype(bf16), expand[...]
            ).astype(bf16)
        for e in range(1, parts):
            to_owner(b, e).start()

    for b in range(bricks):
        span = slice(b * VOX, (b + 1) * VOX)
        pre = comp[own_rows, span].astype(f32)
        for e in range(1, parts):
            to_owner(b, e).wait_recv()
            pre = pre + sum_in[e, :, span].astype(f32)
        pre = pre * masks[b]
        gate = jax.nn.sigmoid(pre)
        act[:, span] = (pre * gate).astype(bf16)
        gates[own_rows, span] = (
            cot[:, b, :].astype(f32) * masks[b] * gate * (1.0 + pre * (1.0 - gate))
        ).astype(bf16)
        for e in range(1, parts):
            to_all(b, e).start()

    for b in range(bricks):
        for e in range(1, parts):
            to_all(b, e).wait_recv()
        for t in range(TILES):
            i = b * TILES + t
            value = nn_dot(gates[:, i * LANES : (i + 1) * LANES], expand[...]).astype(bf16)
            for u in range(3):
                at = b * cube + (u + 2 * t) * LANES
                window[u * total : (u + 1) * total, at : at + 2 * LANES] = value

    def chunk_rows(index):
        return pl.ds(pl.multiple_of(index * chunk, 16), chunk)

    def reduce_copy(d):
        peer = lax.rem(me + d, groups)
        kept = jnp.minimum(peer, owners - 1)
        return peer, pltpu.make_async_remote_copy(
            src_ref=gw_send.at[chunk_rows(kept)], dst_ref=gw_in.at[d],
            send_sem=red_s.at[d], recv_sem=red_r.at[d],
            device_id=(peer, mine), device_id_type=MESH,
        )

    kept_me = jnp.minimum(me, owners - 1)

    def share_copy(d):
        peer = lax.rem(me + d, groups)
        span = gw_all.at[chunk_rows(kept_me)]
        return pltpu.make_async_remote_copy(
            src_ref=span, dst_ref=span, send_sem=all_s.at[d], recv_sem=all_r.at[d],
            device_id=(peer, mine), device_id_type=MESH,
        )

    def guarded(flag, action):
        if owners == groups:
            action()
        else:
            pl.when(flag)(action)

    pack = 2 if owners % 2 == 0 else 1
    packs = owners // pack
    for i in range(packs):
        first = lax.rem(me // pack + i + 1, packs) * pack
        span = pl.ds(pl.multiple_of(first * chunk, 16), pack * chunk)
        value = None
        for b in range(bricks):
            term = nt_dot(
                stacked[span, b * wide : (b + 1) * wide],
                window[total : 2 * total, b * cube + LANES : b * cube + LANES + wide],
            )
            value = term if value is None else value + term
        gw_own[span, :] = value
        gw_send[span, :] = value.astype(bf16)
        for c in range(pack):
            copy = reduce_copy(lax.rem(first + c - me + groups, groups))[1]
            if groups == owners and i < packs - 1:
                copy.start()
            else:
                pl.when(first + c != me)(copy.start)

    for i in range(length // (2 * LANES)):
        span = slice(2 * i * LANES, 2 * (i + 1) * LANES)
        prod[:, span] = nn_dot(w_wide[...], window[:, span])
    spread = prod[0:width, :]
    for n in range(1, 9):
        spread = spread + pltpu.roll(prod[n * width : (n + 1) * width, :], shifts[n], axis=1)
    padded[...] = spread

    pieces = []
    blank = jnp.zeros((width, LANES), f32)
    for b in range(bricks):
        for t in range(TILES):
            at = b * cube + (2 * t + 1) * LANES
            pieces.append(padded[:, at : at + 2 * LANES])
    for b in range(bricks):
        pieces.append(jnp.concatenate([blank, padded[:, b * cube : b * cube + LANES]], axis=1))
    for b in range(bricks):
        at = (b + 1) * cube - LANES
        pieces.append(jnp.concatenate([padded[:, at : at + LANES], blank], axis=1))
    rims = jnp.concatenate(pieces, axis=0).astype(bf16)

    whole = TILES * width
    own = [jnp.zeros((whole, LANES), f32) for _ in range(bricks)]
    own_end = {(b, x): blank for b in range(bricks) for x in (-1, 1)}
    slots = [jnp.zeros((whole if a == 0 else width, LANES), f32) for a, _ in tile_moves]

    def picked(index, wanted, value):
        return jnp.where(jnp.full(value.shape, index, jnp.int32) == wanted, value, 0.0)

    for n, (y, z) in enumerate(plane_offsets):
        folded = nt_dot(rims, place[n * LANES : (n + 1) * LANES, :])
        for x in (-1, 0, 1):
            slot = None if (x, y) == (0, 0) else tile_moves.index((x, y))
            for b in range(bricks):
                if x == 0:
                    piece = folded[b * whole : (b + 1) * whole]
                else:
                    at = ends + (b if x == -1 else bricks + b) * width
                    piece = folded[at : at + width]
                if (x, y, z) == (0, 0, 0):
                    own[b] = own[b] + piece
                    continue
                index = near[b, neighbour_slot(x, y, z)]
                for c in range(bricks):
                    term = picked(index, c, piece)
                    if x == 0:
                        own[c] = own[c] + term
                    else:
                        own_end[c, x] = own_end[c, x] + term
                if slot is not None:
                    slots[slot] = slots[slot] + picked(index, bricks + slot, piece)
    for k, (a, _) in enumerate(tile_moves):
        if a == 0:
            backbox[k] = slots[k].astype(bf16).reshape(TILES, width, LANES)
        else:
            backbox[k, tile_of(a)] = slots[k].astype(bf16)
        start_if(ahead[k], back[k])

    def add_up():
        value = gw_own[chunk_rows(kept_me), :]
        for d in range(1, groups):
            reduce_copy(d)[1].wait_recv()
            value = value + gw_in[d].astype(f32)
        gw_all[chunk_rows(kept_me), :] = (value * scale).astype(bf16)
        for d in range(1, groups):
            share_copy(d).start()

    guarded(me < owners, add_up)

    for k in range(8):
        arrived_if(behind[k], back[k])
    for b in range(bricks):
        for t in range(TILES):
            value = own[b][t * width : (t + 1) * width]
            for x in (-1, 1):
                if t == tile_of(x):
                    value = value + own_end[b, x]
            for k, (a, _) in enumerate(tile_moves):
                if a == 0 or t == tile_of(a):
                    value = value + picked(sends[0, k], b, back_in[k, t].astype(f32))
            at = b * VOX + t * LANES
            grad_feat[:, at : at + LANES] = (
                value * masks[b][:, t * LANES : (t + 1) * LANES]
            ).astype(bf16)

    for d in range(1, groups):
        source = lax.rem(me + groups - d, groups)
        guarded(source < owners, share_copy(d).wait_recv)
    grad_w[...] = gw_all[0:rows_w, :].astype(f32)

    for k in range(8):
        sent_if(behind[k], forth[k])
        sent_if(ahead[k], back[k])
    for b in range(bricks):
        for e in range(1, parts):
            to_owner(b, e).wait_send()
            to_all(b, e).wait_send()
    for d in range(1, groups):
        peer, copy = reduce_copy(d)
        guarded(peer < owners, copy.wait_send)
        guarded(me < owners, share_copy(d).wait_send)


def on_device(features, mask_packed, neighbours, send_list, weights, cotangent):
    groups, parts = lax.axis_size("space"), lax.axis_size("chan")
    width, bricks = features.shape[0], features.shape[1]
    total = weights.shape[2]
    rows_w = 27 * width
    chunk, owners = plan_chunks(rows_w, groups)
    rows_k = -(-max(rows_w, owners * chunk) // LANES) * LANES
    wide, cube = BRICK * LANES, PLANES * LANES
    scale = 1.0 / math.sqrt(bricks * groups * VOX)
    f32, bf16 = jnp.float32, jnp.bfloat16
    vmem = pl.BlockSpec(memory_space=pltpu.VMEM)
    smem = pl.BlockSpec(memory_space=pltpu.SMEM)
    dma = pltpu.SemaphoreType.DMA
    act, grad_feat, grad_w = pl.pallas_call(
        functools.partial(kernel, groups, parts, width, bricks, scale),
        out_shape=(
            jax.ShapeDtypeStruct((width, bricks * VOX), bf16),
            jax.ShapeDtypeStruct((width, bricks * VOX), bf16),
            jax.ShapeDtypeStruct((rows_w, total), f32),
        ),
        in_specs=[smem, smem, smem, vmem, vmem, vmem],
        out_specs=(vmem, vmem, vmem),
        scratch_shapes=[
            pltpu.VMEM((bricks + 9, TILES, width, LANES), bf16),
            pltpu.VMEM((8, TILES, width, LANES), bf16),
            pltpu.VMEM((9 * LANES, 2 * LANES), bf16),
            pltpu.VMEM((LANES, 2 * LANES), bf16),
            pltpu.VMEM((total, rows_k), bf16),
            pltpu.VMEM((9 * width, 3 * total), bf16),
            pltpu.VMEM((width, bricks * cube), f32),
            pltpu.VMEM((rows_k, bricks * wide), bf16),
            pltpu.VMEM((total, bricks * VOX), bf16),
            pltpu.VMEM((parts, width, bricks * VOX), bf16),
            pltpu.VMEM((total, bricks * VOX), bf16),
            pltpu.VMEM((3 * total, bricks * cube), bf16),
            pltpu.VMEM((9 * width, bricks * cube), f32),
            pltpu.VMEM((8, TILES, width, LANES), bf16),
            pltpu.VMEM((8, TILES, width, LANES), bf16),
            pltpu.VMEM((owners * chunk, total), f32),
            pltpu.VMEM((owners * chunk, total), bf16),
            pltpu.VMEM((groups, chunk, total), bf16),
            pltpu.VMEM((owners * chunk, total), bf16),
            dma((8,)), dma((8,)), dma((8,)), dma((8,)),
            dma((bricks, parts)), dma((bricks, parts)), dma((bricks, parts)), dma((bricks, parts)),
            dma((groups,)), dma((groups,)), dma((groups,)), dma((groups,)),
        ],
        compiler_params=pltpu.CompilerParams(
            collective_id=0, has_side_effects=True, vmem_limit_bytes=40 * 2**20
        ),
    )(
        mask_packed, neighbours, send_list.reshape(1, 8),
        features, weights.reshape(rows_w, total), cotangent,
    )
    shape = (width, bricks, VOX)
    return act.reshape(shape), grad_feat.reshape(shape), grad_w.reshape(27, width, total)


def solution(mesh):
    return jax.shard_map(
        on_device,
        mesh=mesh,
        in_specs=(
            P("chan", "space", None),
            P("space", None),
            P("space", None),
            P("space", None, None),
            P(None, "chan", None),
            P("chan", "space", None),
        ),
        out_specs=(P("chan", "space", None), P("chan", "space", None), P(None, "chan", None)),
        check_vma=False,
    )
```

```python
import functools
import math

import jax
import jax.numpy as jnp
from jax import lax
from jax.experimental import pallas as pl
from jax.experimental.pallas import tpu as pltpu
from jax.sharding import PartitionSpec as P

BRICK = 8
VOX = 512
LANES = 128
TILES = VOX // LANES
PLANES = BRICK + 2
MESH = pl.DeviceIdType.MESH

tile_moves = [(a, b) for a in (-1, 0, 1) for b in (-1, 0, 1) if (a, b) != (0, 0)]
tile_steps = [a * 4 + b for a, b in tile_moves]
plane_offsets = [(y, z) for y in (-1, 0, 1) for z in (-1, 0, 1)]


def neighbour_slot(along_x, along_y, along_z):
    linear = (along_x + 1) * 9 + (along_y + 1) * 3 + (along_z + 1)
    return linear if linear < 13 else linear - 1


def tile_of(along_x):
    return TILES - 1 if along_x == -1 else 0


def plan_chunks(rows, groups):
    chunk = -(-rows // groups)
    chunk = -(-chunk // 16) * 16
    return chunk, -(-rows // chunk)


def nt_dot(left, right):
    return lax.dot_general(
        left, right, (((1,), (1,)), ((), ())), preferred_element_type=jnp.float32
    )


def nn_dot(left, right):
    return jnp.dot(left, right, preferred_element_type=jnp.float32)


def kernel(
    groups, parts, width, bricks, scale,
    packed_in, near_in, sends_in, feat_in, w_in, cot_in,
    act_out, grad_feat_out, grad_w_out,
    packed, near, sends, feat, w, cot, act, grad_feat, grad_w, in_s, out_s,
    table, outbox, place, expand, w_turned, w_wide, padded, stacked, comp, mate_in, halves, cross_in, cots, gates,
    window, prod, backbox, back_in, gw_own, gw_send, gw_in, gw_all,
    halo_s, halo_r, back_s, back_r, mate_s, mate_r, cross_s, cross_r, gate_s, gate_r, cot_s, cot_r, red_s, red_r, all_s, all_r,
):
    me, mine = lax.axis_index("space"), lax.axis_index("chan")
    total = parts * width
    rows_w = 27 * width
    chunk, owners = plan_chunks(rows_w, groups)
    wide = BRICK * LANES
    cube = PLANES * LANES
    f32, bf16 = jnp.float32, jnp.bfloat16

    fetches = [
        pltpu.make_async_copy(source, target, in_s.at[i])
        for i, (source, target) in enumerate(
            (
                (packed_in, packed), (feat_in, feat), (sends_in, sends), (near_in, near),
                (cot_in, cot), (w_in, w),
            )
        )
    ]
    for fetch in fetches:
        fetch.start()
    level, low = mine // 2, lax.rem(mine, 2)
    mate, across = mine + 1 - 2 * low, lax.rem(mine + 2, 4)

    barrier = pltpu.get_barrier_semaphore()
    for d in range(1, groups):
        pl.semaphore_signal(
            barrier, inc=1, device_id=(lax.rem(me + d, groups), mine), device_id_type=MESH
        )
    for peer in (mate, across):
        pl.semaphore_signal(barrier, inc=1, device_id=(me, peer), device_id_type=MESH)
    for fetch in fetches[:3]:
        fetch.wait()

    lane = lax.broadcasted_iota(jnp.int32, (1, VOX), 1)
    masks = []
    for b in range(bricks):
        word = jnp.zeros((1, VOX), jnp.int32)
        for i in range(VOX // 32):
            word = jnp.where((lane >> 5) == i, packed[b, i], word)
        masks.append((lax.shift_right_logical(word, lane & 31) & 1).astype(f32))

    masked = [
        feat[:, b, :].astype(f32) * masks[b] for b in range(bricks)
    ]
    for b in range(bricks):
        for t in range(TILES):
            table[b, t] = masked[b][:, t * LANES : (t + 1) * LANES].astype(bf16)
    table[bricks + 8] = jnp.zeros((TILES, width, LANES), bf16)
    for k, (a, _) in enumerate(tile_moves):
        chosen = jnp.full((width, LANES), sends[0, k], jnp.int32)
        for t in range(TILES) if a == 0 else (tile_of(a),):
            value = jnp.zeros((width, LANES), f32)
            for b in range(bricks):
                value = jnp.where(chosen == b, masked[b][:, t * LANES : (t + 1) * LANES], value)
            outbox[k, t] = value.astype(bf16)

    pl.semaphore_wait(barrier, groups - 1 + 2)

    tile_a, tile_b = me // 4, lax.rem(me, 4)

    def inside(a, b):
        return (
            (tile_a + a >= 0) & (tile_a + a < groups // 4) & (tile_b + b >= 0) & (tile_b + b < 4)
        )

    def halo(k, box, rows, base, send, recv, sign):
        a, _ = tile_moves[k]
        if a == 0:
            source, target = box.at[k], rows.at[base + k]
        else:
            source, target = box.at[k, tile_of(a)], rows.at[base + k, tile_of(a)]
        peer = jnp.clip(me + sign * tile_steps[k], 0, groups - 1)
        return pltpu.make_async_remote_copy(
            src_ref=source, dst_ref=target, send_sem=send.at[k], recv_sem=recv.at[k],
            device_id=(peer, mine), device_id_type=MESH,
        )

    forth = [halo(k, outbox, table, bricks, halo_s, halo_r, -1) for k in range(8)]
    back = [halo(k, backbox, back_in, 0, back_s, back_r, 1) for k in range(8)]
    ahead = [inside(a, b) for a, b in tile_moves]
    behind = [inside(-a, -b) for a, b in tile_moves]

    def start_if(flag, copy):
        @pl.when(flag)
        def _():
            copy.start()

    def sent_if(flag, copy):
        @pl.when(flag)
        def _():
            copy.wait_send()

    def arrived_if(flag, copy):
        @pl.when(flag)
        def _():
            copy.wait_recv()

    for k in range(8):
        start_if(behind[k], forth[k])

    for fetch in fetches[3:]:
        fetch.wait()
    for b in range(bricks):
        cots[level, :, b * VOX : (b + 1) * VOX] = cot[:, b, :]
    cot_copy = pltpu.make_async_remote_copy(
        src_ref=cots.at[level], dst_ref=cots.at[level], send_sem=cot_s.at[0],
        recv_sem=cot_r.at[0], device_id=(me, across), device_id_type=MESH,
    )
    cot_copy.start()

    row = lax.broadcasted_iota(jnp.int32, (LANES, 2 * LANES), 0)
    col = lax.broadcasted_iota(jnp.int32, (LANES, 2 * LANES), 1)
    half, at_y, at_z = row >> 6, (row >> 3) & 7, row & 7
    goal = half * LANES + (at_y + 1) * PLANES + (at_z + 1)
    side_y = {-1: at_y == BRICK - 1, 1: at_y == 0}
    side_z = {-1: at_z == BRICK - 1, 1: at_z == 0}
    for n, (y, z) in enumerate(plane_offsets):
        hit = col == goal + (BRICK * PLANES * y + BRICK * z)
        if y != 0:
            hit = hit & side_y[y]
        if z != 0:
            hit = hit & side_z[z]
        place[n * LANES : (n + 1) * LANES, :] = jnp.where(hit, 1.0, 0.0).astype(bf16)
    expand[...] = jnp.where(col == goal - (PLANES + 1), 1.0, 0.0).astype(bf16)

    rows_k = w_turned.shape[1]
    for c in range(rows_k // LANES):
        have = min(rows_w - c * LANES, LANES)
        block = w[c * LANES : c * LANES + have, :].astype(f32)
        if have < LANES:
            block = jnp.concatenate([block, jnp.zeros((LANES - have, total), f32)], axis=0)
        w_turned[:, c * LANES : (c + 1) * LANES] = block.T.astype(bf16)
    for n in range(9):
        for u in range(3):
            w_wide[n * width : (n + 1) * width, u * total : (u + 1) * total] = w[
                (u * 9 + n) * width : (u * 9 + n + 1) * width, :
            ]
    if rows_k > rows_w:
        stacked[rows_w:, :] = jnp.zeros((rows_k - rows_w, bricks * wide), bf16)
    for u in range(3):
        for b in range(bricks):
            for px in range(PLANES):
                if not u <= px < u + BRICK:
                    window[
                        u * total : (u + 1) * total,
                        b * cube + px * LANES : b * cube + (px + 1) * LANES,
                    ] = jnp.zeros((total, LANES), bf16)

    for k in range(8):
        arrived_if(ahead[k], forth[k])

    columns = []
    for n, (y, z) in enumerate(plane_offsets):
        pieces = []
        for b in range(bricks):
            source = b if (y, z) == (0, 0) else near[b, neighbour_slot(0, y, z)]
            pieces.append(table[source].reshape(TILES * width, LANES))
        for x in (-1, 1):
            for b in range(bricks):
                pieces.append(table[near[b, neighbour_slot(x, y, z)], tile_of(x)])
        columns.append(jnp.concatenate(pieces, axis=0))
    built = nn_dot(jnp.concatenate(columns, axis=1), place[...])
    ends = bricks * TILES * width
    for b in range(bricks):
        base = b * cube
        first = ends + b * width
        last = ends + (bricks + b) * width
        padded[:, base : base + LANES] = built[first : first + width, LANES:]
        padded[:, base + cube - LANES : base + cube] = built[last : last + width, :LANES]
        for t in range(TILES):
            at = (b * TILES + t) * width
            padded[:, base + (2 * t + 1) * LANES : base + (2 * t + 3) * LANES] = built[
                at : at + width, :
            ]

    length = bricks * cube
    shifts = [(y + 1) * PLANES + (z + 1) for y, z in plane_offsets]
    for n in range(9):
        value = padded[...]
        if shifts[n]:
            value = pltpu.roll(value, length - shifts[n], axis=1)
        value = value.astype(bf16)
        for u in range(3):
            for b in range(bricks):
                stacked[
                    (u * 9 + n) * width : (u * 9 + n + 1) * width, b * wide : (b + 1) * wide
                ] = value[:, b * cube + u * LANES : b * cube + u * LANES + wide]

    def chan_copy(source, target, send, recv, peer):
        return pltpu.make_async_remote_copy(
            src_ref=source, dst_ref=target, send_sem=send, recv_sem=recv,
            device_id=(me, peer), device_id_type=MESH,
        )

    spans = [pl.ds(b * VOX, VOX) for b in range(bricks)]
    to_mate = [
        chan_copy(
            comp.at[:, 1 - low, :, spans[b]], mate_in.at[:, :, spans[b]],
            mate_s.at[b], mate_r.at[b], mate,
        )
        for b in range(bricks)
    ]
    to_across = [
        chan_copy(
            halves.at[:, :, spans[b]], cross_in.at[:, :, spans[b]],
            cross_s.at[b], cross_r.at[b], across,
        )
        for b in range(bricks)
    ]
    to_both = [
        chan_copy(
            gates.at[:, low, :, spans[b]], gates.at[:, low, :, spans[b]],
            gate_s.at[b], gate_r.at[b], mate,
        )
        for b in range(bricks)
    ]

    for b in range(bricks):
        for t in range(TILES):
            i = b * TILES + t
            part = nn_dot(w_turned[...], stacked[:, 2 * i * LANES : 2 * (i + 1) * LANES])
            comp[:, :, :, i * LANES : (i + 1) * LANES] = (
                nt_dot(part.astype(bf16), expand[...])
                .astype(bf16)
                .reshape(2, 2, width, LANES)
            )
        to_mate[b].start()

    for b in range(bricks):
        to_mate[b].wait_recv()
        halves[:, :, spans[b]] = (
            comp[:, low, :, spans[b]].astype(f32) + mate_in[:, :, spans[b]].astype(f32)
        ).astype(bf16)
        to_across[b].start()

    cot_copy.wait_recv()
    for b in range(bricks):
        to_across[b].wait_recv()
        for h in range(2):
            pre = halves[h, :, spans[b]].astype(f32) + cross_in[h, :, spans[b]].astype(f32)
            pre = pre * masks[b]
            gate = jax.nn.sigmoid(pre)
            gates[h, low, :, spans[b]] = (
                cots[h, :, spans[b]].astype(f32) * masks[b] * gate * (1.0 + pre * (1.0 - gate))
            ).astype(bf16)

            @pl.when(level == h)
            def _():
                act[:, b, :] = (pre * gate).astype(bf16)

        to_both[b].start()
    act_copy = pltpu.make_async_copy(act, act_out, out_s.at[0])
    act_copy.start()

    for b in range(bricks):
        to_both[b].wait_recv()
        for t in range(TILES):
            i = b * TILES + t
            value = gates[:, :, :, i * LANES : (i + 1) * LANES].reshape(total, LANES)
            value = nn_dot(value, expand[...]).astype(bf16)
            for u in range(3):
                at = b * cube + (u + 2 * t) * LANES
                window[u * total : (u + 1) * total, at : at + 2 * LANES] = value

    def chunk_rows(index):
        return pl.ds(pl.multiple_of(index * chunk, 16), chunk)

    def reduce_copy(d):
        peer = lax.rem(me + d, groups)
        kept = jnp.minimum(peer, owners - 1)
        return peer, pltpu.make_async_remote_copy(
            src_ref=gw_send.at[chunk_rows(kept)], dst_ref=gw_in.at[d],
            send_sem=red_s.at[d], recv_sem=red_r.at[d],
            device_id=(peer, mine), device_id_type=MESH,
        )

    kept_me = jnp.minimum(me, owners - 1)

    def share_copy(d):
        peer = lax.rem(me + d, groups)
        span = gw_all.at[chunk_rows(kept_me)]
        return pltpu.make_async_remote_copy(
            src_ref=span, dst_ref=span, send_sem=all_s.at[d], recv_sem=all_r.at[d],
            device_id=(peer, mine), device_id_type=MESH,
        )

    def guarded(flag, action):
        if owners == groups:
            action()
        else:
            pl.when(flag)(action)

    pack = 2 if owners % 2 == 0 else 1
    packs = owners // pack
    for i in range(packs):
        first = lax.rem(me // pack + i + 1, packs) * pack
        span = pl.ds(pl.multiple_of(first * chunk, 16), pack * chunk)
        value = None
        for b in range(bricks):
            term = nt_dot(
                stacked[span, b * wide : (b + 1) * wide],
                window[total : 2 * total, b * cube + LANES : b * cube + LANES + wide],
            )
            value = term if value is None else value + term
        gw_own[span, :] = value
        gw_send[span, :] = value.astype(bf16)
        for c in range(pack):
            copy = reduce_copy(lax.rem(first + c - me + groups, groups))[1]
            if groups == owners and i < packs - 1:
                copy.start()
            else:
                pl.when(first + c != me)(copy.start)

    for i in range(length // (2 * LANES)):
        span = slice(2 * i * LANES, 2 * (i + 1) * LANES)
        prod[:, span] = nn_dot(w_wide[...], window[:, span])
    spread = prod[0:width, :]
    for n in range(1, 9):
        spread = spread + pltpu.roll(prod[n * width : (n + 1) * width, :], shifts[n], axis=1)
    padded[...] = spread

    pieces = []
    blank = jnp.zeros((width, LANES), f32)
    for b in range(bricks):
        for t in range(TILES):
            at = b * cube + (2 * t + 1) * LANES
            pieces.append(padded[:, at : at + 2 * LANES])
    for b in range(bricks):
        pieces.append(jnp.concatenate([blank, padded[:, b * cube : b * cube + LANES]], axis=1))
    for b in range(bricks):
        at = (b + 1) * cube - LANES
        pieces.append(jnp.concatenate([padded[:, at : at + LANES], blank], axis=1))
    rims = jnp.concatenate(pieces, axis=0).astype(bf16)

    whole = TILES * width
    own = [jnp.zeros((whole, LANES), f32) for _ in range(bricks)]
    own_end = {(b, x): blank for b in range(bricks) for x in (-1, 1)}
    slots = [jnp.zeros((whole if a == 0 else width, LANES), f32) for a, _ in tile_moves]

    def picked(index, wanted, value):
        return jnp.where(jnp.full(value.shape, index, jnp.int32) == wanted, value, 0.0)

    for n, (y, z) in enumerate(plane_offsets):
        folded = nt_dot(rims, place[n * LANES : (n + 1) * LANES, :])
        for x in (-1, 0, 1):
            slot = None if (x, y) == (0, 0) else tile_moves.index((x, y))
            for b in range(bricks):
                if x == 0:
                    piece = folded[b * whole : (b + 1) * whole]
                else:
                    at = ends + (b if x == -1 else bricks + b) * width
                    piece = folded[at : at + width]
                if (x, y, z) == (0, 0, 0):
                    own[b] = own[b] + piece
                    continue
                index = near[b, neighbour_slot(x, y, z)]
                for c in range(bricks):
                    term = picked(index, c, piece)
                    if x == 0:
                        own[c] = own[c] + term
                    else:
                        own_end[c, x] = own_end[c, x] + term
                if slot is not None:
                    slots[slot] = slots[slot] + picked(index, bricks + slot, piece)
    for k, (a, _) in enumerate(tile_moves):
        if a == 0:
            backbox[k] = slots[k].astype(bf16).reshape(TILES, width, LANES)
        else:
            backbox[k, tile_of(a)] = slots[k].astype(bf16)
        start_if(ahead[k], back[k])

    def add_up():
        value = gw_own[chunk_rows(kept_me), :]
        for d in range(1, groups):
            reduce_copy(d)[1].wait_recv()
            value = value + gw_in[d].astype(f32)
        gw_all[chunk_rows(kept_me), :] = (value * scale).astype(bf16)
        for d in range(1, groups):
            share_copy(d).start()

    guarded(me < owners, add_up)

    for k in range(8):
        arrived_if(behind[k], back[k])
    for b in range(bricks):
        rows = []
        for t in range(TILES):
            value = own[b][t * width : (t + 1) * width]
            for x in (-1, 1):
                if t == tile_of(x):
                    value = value + own_end[b, x]
            for k, (a, _) in enumerate(tile_moves):
                if a == 0 or t == tile_of(a):
                    value = value + picked(sends[0, k], b, back_in[k, t].astype(f32))
            rows.append((value * masks[b][:, t * LANES : (t + 1) * LANES]).astype(bf16))
        grad_feat[:, b, :] = jnp.concatenate(rows, axis=1)
    feat_copy = pltpu.make_async_copy(grad_feat, grad_feat_out, out_s.at[1])
    feat_copy.start()

    for d in range(1, groups):
        source = lax.rem(me + groups - d, groups)
        guarded(source < owners, share_copy(d).wait_recv)
    grad_w[...] = gw_all[0:rows_w, :].astype(f32)
    w_copy = pltpu.make_async_copy(grad_w, grad_w_out, out_s.at[2])
    w_copy.start()

    for k in range(8):
        sent_if(behind[k], forth[k])
        sent_if(ahead[k], back[k])
    for b in range(bricks):
        to_mate[b].wait_send()
        to_across[b].wait_send()
        to_both[b].wait_send()
    cot_copy.wait_send()
    for d in range(1, groups):
        peer, copy = reduce_copy(d)
        guarded(peer < owners, copy.wait_send)
        guarded(me < owners, share_copy(d).wait_send)
    act_copy.wait()
    feat_copy.wait()
    w_copy.wait()


def hand_over(*refs):
    sources, targets, sem = refs[:3], refs[3:6], refs[6]
    copies = [
        pltpu.make_async_copy(sources[i], targets[i], sem.at[i]) for i in range(3)
    ]
    for copy in copies:
        copy.start()
    for copy in copies:
        copy.wait()


def on_device(features, mask_packed, neighbours, send_list, weights, cotangent):
    groups, parts = lax.axis_size("space"), lax.axis_size("chan")
    width, bricks = features.shape[0], features.shape[1]
    total = weights.shape[2]
    rows_w = 27 * width
    chunk, owners = plan_chunks(rows_w, groups)
    rows_k = -(-max(rows_w, owners * chunk) // LANES) * LANES
    wide, cube = BRICK * LANES, PLANES * LANES
    scale = 1.0 / math.sqrt(bricks * groups * VOX)
    f32, bf16 = jnp.float32, jnp.bfloat16
    dma = pltpu.SemaphoreType.DMA
    outputs = (
        jax.ShapeDtypeStruct((width, bricks, VOX), bf16),
        jax.ShapeDtypeStruct((width, bricks, VOX), bf16),
        jax.ShapeDtypeStruct((rows_w, total), f32),
    )
    anywhere = pl.BlockSpec(memory_space=pl.ANY)
    results = pl.pallas_call(
        functools.partial(kernel, groups, parts, width, bricks, scale),
        out_shape=outputs,
        in_specs=[anywhere] * 6,
        out_specs=(anywhere,) * 3,
        scratch_shapes=[
            pltpu.SMEM((bricks, VOX // 32), jnp.int32),
            pltpu.SMEM((bricks, 26), jnp.int32),
            pltpu.SMEM((1, 8), jnp.int32),
            pltpu.VMEM((width, bricks, VOX), bf16),
            pltpu.VMEM((rows_w, total), bf16),
            pltpu.VMEM((width, bricks, VOX), bf16),
            pltpu.VMEM((width, bricks, VOX), bf16),
            pltpu.VMEM((width, bricks, VOX), bf16),
            pltpu.VMEM((rows_w, total), f32),
            dma((6,)), dma((3,)),
            pltpu.VMEM((bricks + 9, TILES, width, LANES), bf16),
            pltpu.VMEM((8, TILES, width, LANES), bf16),
            pltpu.VMEM((9 * LANES, 2 * LANES), bf16),
            pltpu.VMEM((LANES, 2 * LANES), bf16),
            pltpu.VMEM((total, rows_k), bf16),
            pltpu.VMEM((9 * width, 3 * total), bf16),
            pltpu.VMEM((width, bricks * cube), f32),
            pltpu.VMEM((rows_k, bricks * wide), bf16),
            pltpu.VMEM((2, 2, width, bricks * VOX), bf16),
            pltpu.VMEM((2, width, bricks * VOX), bf16),
            pltpu.VMEM((2, width, bricks * VOX), bf16),
            pltpu.VMEM((2, width, bricks * VOX), bf16),
            pltpu.VMEM((2, width, bricks * VOX), bf16),
            pltpu.VMEM((2, 2, width, bricks * VOX), bf16),
            pltpu.VMEM((3 * total, bricks * cube), bf16),
            pltpu.VMEM((9 * width, bricks * cube), f32),
            pltpu.VMEM((8, TILES, width, LANES), bf16),
            pltpu.VMEM((8, TILES, width, LANES), bf16),
            pltpu.VMEM((owners * chunk, total), f32),
            pltpu.VMEM((owners * chunk, total), bf16),
            pltpu.VMEM((groups, chunk, total), bf16),
            pltpu.VMEM((owners * chunk, total), bf16),
            dma((8,)), dma((8,)), dma((8,)), dma((8,)),
            dma((bricks,)), dma((bricks,)), dma((bricks,)), dma((bricks,)),
            dma((bricks,)), dma((bricks,)), dma((1,)), dma((1,)),
            dma((groups,)), dma((groups,)), dma((groups,)), dma((groups,)),
        ],
        compiler_params=pltpu.CompilerParams(
            collective_id=0, has_side_effects=True, vmem_limit_bytes=60 * 2**20
        ),
    )(
        mask_packed, neighbours, send_list.reshape(1, 8),
        features, weights.reshape(rows_w, total), cotangent,
    )
    act, grad_feat, grad_w = pl.pallas_call(
        hand_over,
        out_shape=outputs,
        in_specs=[anywhere] * 3,
        out_specs=(anywhere,) * 3,
        scratch_shapes=[dma((3,))],
        compiler_params=pltpu.CompilerParams(vmem_limit_bytes=60 * 2**20),
    )(*results)
    return act, grad_feat, grad_w.reshape(27, width, total)


def solution(mesh):
    return jax.shard_map(
        on_device,
        mesh=mesh,
        in_specs=(
            P("chan", "space", None),
            P("space", None),
            P("space", None),
            P("space", None, None),
            P(None, "chan", None),
            P("chan", "space", None),
        ),
        out_specs=(P("chan", "space", None), P("chan", "space", None), P(None, "chan", None)),
        check_vma=False,
    )
```

```python
import functools
import math

import jax
import jax.numpy as jnp
from jax import lax
from jax.experimental import pallas as pl
from jax.experimental.pallas import tpu as pltpu
from jax.sharding import PartitionSpec as P

BRICK = 8
VOX = 512
LANES = 128
TILES = VOX // LANES
PLANES = BRICK + 2
MESH = pl.DeviceIdType.MESH

tile_moves = [(a, b) for a in (-1, 0, 1) for b in (-1, 0, 1) if (a, b) != (0, 0)]
tile_steps = [a * 4 + b for a, b in tile_moves]
plane_offsets = [(y, z) for y in (-1, 0, 1) for z in (-1, 0, 1)]


def neighbour_slot(along_x, along_y, along_z):
    linear = (along_x + 1) * 9 + (along_y + 1) * 3 + (along_z + 1)
    return linear if linear < 13 else linear - 1


def tile_of(along_x):
    return TILES - 1 if along_x == -1 else 0


def plan_chunks(rows, groups):
    chunk = -(-rows // groups)
    chunk = -(-chunk // 16) * 16
    return chunk, -(-rows // chunk)


def nt_dot(left, right):
    return lax.dot_general(
        left, right, (((1,), (1,)), ((), ())), preferred_element_type=jnp.float32
    )


def nn_dot(left, right):
    return jnp.dot(left, right, preferred_element_type=jnp.float32)


def kernel(
    groups, parts, width, bricks, scale,
    packed_in, near_in, sends_in, feat_in, w_in, cot_in,
    act_out, grad_feat_out, gw_out,
    packed, near, sends, feat, w, cot, act, grad_feat, gw_all, in_s, out_s,
    table, outbox, place, expand, w_turned, w_wide, padded, stacked, comp, mate_in, halves, cross_in, cots, gates,
    window, prod, backbox, back_in, gw_own, gw_send, gw_in,
    halo_s, halo_r, back_s, back_r, mate_s, mate_r, cross_s, cross_r, gate_s, gate_r, cot_s, cot_r, red_s, red_r, all_s, all_r,
):
    me, mine = lax.axis_index("space"), lax.axis_index("chan")
    total = parts * width
    rows_w = 27 * width
    chunk, owners = plan_chunks(rows_w, groups)
    wide = BRICK * LANES
    cube = PLANES * LANES
    f32, bf16 = jnp.float32, jnp.bfloat16

    fetches = [
        pltpu.make_async_copy(source, target, in_s.at[i])
        for i, (source, target) in enumerate(
            (
                (packed_in, packed), (feat_in, feat), (sends_in, sends), (near_in, near),
                (cot_in, cot), (w_in, w),
            )
        )
    ]
    for fetch in fetches:
        fetch.start()
    level, low = mine // 2, lax.rem(mine, 2)
    mate, across = mine + 1 - 2 * low, lax.rem(mine + 2, 4)

    barrier = pltpu.get_barrier_semaphore()
    for d in range(1, groups):
        pl.semaphore_signal(
            barrier, inc=1, device_id=(lax.rem(me + d, groups), mine), device_id_type=MESH
        )
    for peer in (mate, across):
        pl.semaphore_signal(barrier, inc=1, device_id=(me, peer), device_id_type=MESH)

    row = lax.broadcasted_iota(jnp.int32, (LANES, 2 * LANES), 0)
    col = lax.broadcasted_iota(jnp.int32, (LANES, 2 * LANES), 1)
    half, at_y, at_z = row >> 6, (row >> 3) & 7, row & 7
    goal = half * LANES + (at_y + 1) * PLANES + (at_z + 1)
    side_y = {-1: at_y == BRICK - 1, 1: at_y == 0}
    side_z = {-1: at_z == BRICK - 1, 1: at_z == 0}
    for n, (y, z) in enumerate(plane_offsets):
        hit = col == goal + (BRICK * PLANES * y + BRICK * z)
        if y != 0:
            hit = hit & side_y[y]
        if z != 0:
            hit = hit & side_z[z]
        place[n * LANES : (n + 1) * LANES, :] = jnp.where(hit, 1.0, 0.0).astype(bf16)
    expand[...] = jnp.where(col == goal - (PLANES + 1), 1.0, 0.0).astype(bf16)

    for fetch in fetches[:3]:
        fetch.wait()

    lane = lax.broadcasted_iota(jnp.int32, (1, VOX), 1)
    masks = []
    for b in range(bricks):
        word = jnp.zeros((1, VOX), jnp.int32)
        for i in range(VOX // 32):
            word = jnp.where((lane >> 5) == i, packed[b, i], word)
        masks.append((lax.shift_right_logical(word, lane & 31) & 1).astype(f32))

    masked = [
        feat[:, b, :].astype(f32) * masks[b] for b in range(bricks)
    ]
    for b in range(bricks):
        for t in range(TILES):
            table[b, t] = masked[b][:, t * LANES : (t + 1) * LANES].astype(bf16)
    table[bricks + 8] = jnp.zeros((TILES, width, LANES), bf16)
    for k, (a, _) in enumerate(tile_moves):
        chosen = jnp.full((width, LANES), sends[0, k], jnp.int32)
        for t in range(TILES) if a == 0 else (tile_of(a),):
            value = jnp.zeros((width, LANES), f32)
            for b in range(bricks):
                value = jnp.where(chosen == b, masked[b][:, t * LANES : (t + 1) * LANES], value)
            outbox[k, t] = value.astype(bf16)

    pl.semaphore_wait(barrier, groups - 1 + 2)

    tile_a, tile_b = me // 4, lax.rem(me, 4)

    def inside(a, b):
        return (
            (tile_a + a >= 0) & (tile_a + a < groups // 4) & (tile_b + b >= 0) & (tile_b + b < 4)
        )

    def halo(k, box, rows, base, send, recv, sign):
        a, _ = tile_moves[k]
        if a == 0:
            source, target = box.at[k], rows.at[base + k]
        else:
            source, target = box.at[k, tile_of(a)], rows.at[base + k, tile_of(a)]
        peer = jnp.clip(me + sign * tile_steps[k], 0, groups - 1)
        return pltpu.make_async_remote_copy(
            src_ref=source, dst_ref=target, send_sem=send.at[k], recv_sem=recv.at[k],
            device_id=(peer, mine), device_id_type=MESH,
        )

    forth = [halo(k, outbox, table, bricks, halo_s, halo_r, -1) for k in range(8)]
    back = [halo(k, backbox, back_in, 0, back_s, back_r, 1) for k in range(8)]
    ahead = [inside(a, b) for a, b in tile_moves]
    behind = [inside(-a, -b) for a, b in tile_moves]

    def start_if(flag, copy):
        @pl.when(flag)
        def _():
            copy.start()

    def sent_if(flag, copy):
        @pl.when(flag)
        def _():
            copy.wait_send()

    def arrived_if(flag, copy):
        @pl.when(flag)
        def _():
            copy.wait_recv()

    for k in range(8):
        start_if(behind[k], forth[k])

    for fetch in fetches[3:]:
        fetch.wait()
    for b in range(bricks):
        cots[level, :, b * VOX : (b + 1) * VOX] = cot[:, b, :]
    cot_copy = pltpu.make_async_remote_copy(
        src_ref=cots.at[level], dst_ref=cots.at[level], send_sem=cot_s.at[0],
        recv_sem=cot_r.at[0], device_id=(me, across), device_id_type=MESH,
    )
    cot_copy.start()

    rows_k = w_turned.shape[1]
    for c in range(rows_k // LANES):
        have = min(rows_w - c * LANES, LANES)
        block = w[c * LANES : c * LANES + have, :].astype(f32)
        if have < LANES:
            block = jnp.concatenate([block, jnp.zeros((LANES - have, total), f32)], axis=0)
        w_turned[:, c * LANES : (c + 1) * LANES] = block.T.astype(bf16)
    for n in range(9):
        for u in range(3):
            w_wide[n * width : (n + 1) * width, u * total : (u + 1) * total] = w[
                (u * 9 + n) * width : (u * 9 + n + 1) * width, :
            ]
    if rows_k > rows_w:
        stacked[rows_w:, :] = jnp.zeros((rows_k - rows_w, bricks * wide), bf16)
    for u in range(3):
        for b in range(bricks):
            for px in range(PLANES):
                if not u <= px < u + BRICK:
                    window[
                        u * total : (u + 1) * total,
                        b * cube + px * LANES : b * cube + (px + 1) * LANES,
                    ] = jnp.zeros((total, LANES), bf16)

    for k in range(8):
        arrived_if(ahead[k], forth[k])

    columns = []
    for n, (y, z) in enumerate(plane_offsets):
        pieces = []
        for b in range(bricks):
            source = b if (y, z) == (0, 0) else near[b, neighbour_slot(0, y, z)]
            pieces.append(table[source].reshape(TILES * width, LANES))
        for x in (-1, 1):
            for b in range(bricks):
                pieces.append(table[near[b, neighbour_slot(x, y, z)], tile_of(x)])
        columns.append(jnp.concatenate(pieces, axis=0))
    built = nn_dot(jnp.concatenate(columns, axis=1), place[...])
    ends = bricks * TILES * width
    for b in range(bricks):
        base = b * cube
        first = ends + b * width
        last = ends + (bricks + b) * width
        padded[:, base : base + LANES] = built[first : first + width, LANES:]
        padded[:, base + cube - LANES : base + cube] = built[last : last + width, :LANES]
        for t in range(TILES):
            at = (b * TILES + t) * width
            padded[:, base + (2 * t + 1) * LANES : base + (2 * t + 3) * LANES] = built[
                at : at + width, :
            ]

    length = bricks * cube
    shifts = [(y + 1) * PLANES + (z + 1) for y, z in plane_offsets]
    for n in range(9):
        value = padded[...]
        if shifts[n]:
            value = pltpu.roll(value, length - shifts[n], axis=1)
        value = value.astype(bf16)
        for u in range(3):
            for b in range(bricks):
                stacked[
                    (u * 9 + n) * width : (u * 9 + n + 1) * width, b * wide : (b + 1) * wide
                ] = value[:, b * cube + u * LANES : b * cube + u * LANES + wide]

    def chan_copy(source, target, send, recv, peer):
        return pltpu.make_async_remote_copy(
            src_ref=source, dst_ref=target, send_sem=send, recv_sem=recv,
            device_id=(me, peer), device_id_type=MESH,
        )

    spans = [pl.ds(b * VOX, VOX) for b in range(bricks)]
    to_mate = [
        chan_copy(
            comp.at[:, 1 - low, :, spans[b]], mate_in.at[:, :, spans[b]],
            mate_s.at[b], mate_r.at[b], mate,
        )
        for b in range(bricks)
    ]
    to_across = [
        chan_copy(
            halves.at[:, :, spans[b]], cross_in.at[:, :, spans[b]],
            cross_s.at[b], cross_r.at[b], across,
        )
        for b in range(bricks)
    ]
    to_both = [
        chan_copy(
            gates.at[:, low, :, spans[b]], gates.at[:, low, :, spans[b]],
            gate_s.at[b], gate_r.at[b], mate,
        )
        for b in range(bricks)
    ]

    for b in range(bricks):
        for t in range(TILES):
            i = b * TILES + t
            part = nn_dot(w_turned[...], stacked[:, 2 * i * LANES : 2 * (i + 1) * LANES])
            comp[:, :, :, i * LANES : (i + 1) * LANES] = (
                nt_dot(part.astype(bf16), expand[...])
                .astype(bf16)
                .reshape(2, 2, width, LANES)
            )
        to_mate[b].start()

    for b in range(bricks):
        to_mate[b].wait_recv()
        halves[:, :, spans[b]] = (
            comp[:, low, :, spans[b]].astype(f32) + mate_in[:, :, spans[b]].astype(f32)
        ).astype(bf16)
        to_across[b].start()

    cot_copy.wait_recv()
    for b in range(bricks):
        to_across[b].wait_recv()
        for h in range(2):
            pre = halves[h, :, spans[b]].astype(f32) + cross_in[h, :, spans[b]].astype(f32)
            pre = pre * masks[b]
            gate = jax.nn.sigmoid(pre)
            gates[h, low, :, spans[b]] = (
                cots[h, :, spans[b]].astype(f32) * masks[b] * gate * (1.0 + pre * (1.0 - gate))
            ).astype(bf16)

            @pl.when(level == h)
            def _():
                act[:, b, :] = (pre * gate).astype(bf16)

        to_both[b].start()
    act_copy = pltpu.make_async_copy(act, act_out, out_s.at[0])
    act_copy.start()

    for b in range(bricks):
        to_both[b].wait_recv()
        for t in range(TILES):
            i = b * TILES + t
            value = gates[:, :, :, i * LANES : (i + 1) * LANES].reshape(total, LANES)
            value = nn_dot(value, expand[...]).astype(bf16)
            for u in range(3):
                at = b * cube + (u + 2 * t) * LANES
                window[u * total : (u + 1) * total, at : at + 2 * LANES] = value

    def chunk_rows(index):
        return pl.ds(pl.multiple_of(index * chunk, 16), chunk)

    def reduce_copy(d):
        peer = lax.rem(me + d, groups)
        kept = jnp.minimum(peer, owners - 1)
        return peer, pltpu.make_async_remote_copy(
            src_ref=gw_send.at[chunk_rows(kept)], dst_ref=gw_in.at[d],
            send_sem=red_s.at[d], recv_sem=red_r.at[d],
            device_id=(peer, mine), device_id_type=MESH,
        )

    kept_me = jnp.minimum(me, owners - 1)

    def share_copy(d):
        peer = lax.rem(me + d, groups)
        span = gw_all.at[chunk_rows(kept_me)]
        return pltpu.make_async_remote_copy(
            src_ref=span, dst_ref=span, send_sem=all_s.at[d], recv_sem=all_r.at[d],
            device_id=(peer, mine), device_id_type=MESH,
        )

    def guarded(flag, action):
        if owners == groups:
            action()
        else:
            pl.when(flag)(action)

    pack = 2 if owners % 2 == 0 else 1
    packs = owners // pack
    for i in range(packs):
        first = lax.rem(me // pack + i + 1, packs) * pack
        span = pl.ds(pl.multiple_of(first * chunk, 16), pack * chunk)
        value = None
        for b in range(bricks):
            term = nt_dot(
                stacked[span, b * wide : (b + 1) * wide],
                window[total : 2 * total, b * cube + LANES : b * cube + LANES + wide],
            )
            value = term if value is None else value + term
        gw_own[span, :] = value
        gw_send[span, :] = value.astype(bf16)
        for c in range(pack):
            copy = reduce_copy(lax.rem(first + c - me + groups, groups))[1]
            if groups == owners and i < packs - 1:
                copy.start()
            else:
                pl.when(first + c != me)(copy.start)

    for i in range(length // (2 * LANES)):
        span = slice(2 * i * LANES, 2 * (i + 1) * LANES)
        prod[:, span] = nn_dot(w_wide[...], window[:, span])
    spread = prod[0:width, :]
    for n in range(1, 9):
        spread = spread + pltpu.roll(prod[n * width : (n + 1) * width, :], shifts[n], axis=1)
    padded[...] = spread

    pieces = []
    blank = jnp.zeros((width, LANES), f32)
    for b in range(bricks):
        for t in range(TILES):
            at = b * cube + (2 * t + 1) * LANES
            pieces.append(padded[:, at : at + 2 * LANES])
    for b in range(bricks):
        pieces.append(jnp.concatenate([blank, padded[:, b * cube : b * cube + LANES]], axis=1))
    for b in range(bricks):
        at = (b + 1) * cube - LANES
        pieces.append(jnp.concatenate([padded[:, at : at + LANES], blank], axis=1))
    rims = jnp.concatenate(pieces, axis=0).astype(bf16)

    whole = TILES * width
    own = [jnp.zeros((whole, LANES), f32) for _ in range(bricks)]
    own_end = {(b, x): blank for b in range(bricks) for x in (-1, 1)}
    slots = [jnp.zeros((whole if a == 0 else width, LANES), f32) for a, _ in tile_moves]

    def picked(index, wanted, value):
        return jnp.where(jnp.full(value.shape, index, jnp.int32) == wanted, value, 0.0)

    for n, (y, z) in enumerate(plane_offsets):
        folded = nt_dot(rims, place[n * LANES : (n + 1) * LANES, :])
        for x in (-1, 0, 1):
            slot = None if (x, y) == (0, 0) else tile_moves.index((x, y))
            for b in range(bricks):
                if x == 0:
                    piece = folded[b * whole : (b + 1) * whole]
                else:
                    at = ends + (b if x == -1 else bricks + b) * width
                    piece = folded[at : at + width]
                if (x, y, z) == (0, 0, 0):
                    own[b] = own[b] + piece
                    continue
                index = near[b, neighbour_slot(x, y, z)]
                for c in range(bricks):
                    term = picked(index, c, piece)
                    if x == 0:
                        own[c] = own[c] + term
                    else:
                        own_end[c, x] = own_end[c, x] + term
                if slot is not None:
                    slots[slot] = slots[slot] + picked(index, bricks + slot, piece)
    for k, (a, _) in enumerate(tile_moves):
        if a == 0:
            backbox[k] = slots[k].astype(bf16).reshape(TILES, width, LANES)
        else:
            backbox[k, tile_of(a)] = slots[k].astype(bf16)
        start_if(ahead[k], back[k])

    def add_up():
        value = gw_own[chunk_rows(kept_me), :]
        for d in range(1, groups):
            reduce_copy(d)[1].wait_recv()
            value = value + gw_in[d].astype(f32)
        gw_all[chunk_rows(kept_me), :] = (value * scale).astype(bf16)
        for d in range(1, groups):
            share_copy(d).start()

    guarded(me < owners, add_up)

    for k in range(8):
        arrived_if(behind[k], back[k])
    for b in range(bricks):
        rows = []
        for t in range(TILES):
            value = own[b][t * width : (t + 1) * width]
            for x in (-1, 1):
                if t == tile_of(x):
                    value = value + own_end[b, x]
            for k, (a, _) in enumerate(tile_moves):
                if a == 0 or t == tile_of(a):
                    value = value + picked(sends[0, k], b, back_in[k, t].astype(f32))
            rows.append((value * masks[b][:, t * LANES : (t + 1) * LANES]).astype(bf16))
        grad_feat[:, b, :] = jnp.concatenate(rows, axis=1)
    feat_copy = pltpu.make_async_copy(grad_feat, grad_feat_out, out_s.at[1])
    feat_copy.start()

    for d in range(1, groups):
        source = lax.rem(me + groups - d, groups)
        guarded(source < owners, share_copy(d).wait_recv)
    gw_copy = pltpu.make_async_copy(gw_all, gw_out, out_s.at[2])
    gw_copy.start()

    for k in range(8):
        sent_if(behind[k], forth[k])
        sent_if(ahead[k], back[k])
    for b in range(bricks):
        to_mate[b].wait_send()
        to_across[b].wait_send()
        to_both[b].wait_send()
    cot_copy.wait_send()
    for d in range(1, groups):
        peer, copy = reduce_copy(d)
        guarded(peer < owners, copy.wait_send)
        guarded(me < owners, share_copy(d).wait_send)
    act_copy.wait()
    feat_copy.wait()
    gw_copy.wait()


def hand_over(*refs):
    sources, targets, held, wide, in_s, out_s = refs[:3], refs[3:6], refs[6:9], refs[9], *refs[10:]
    fetches = [pltpu.make_async_copy(sources[i], held[i], in_s.at[i]) for i in range(3)]
    stores = [
        pltpu.make_async_copy(source, targets[i], out_s.at[i])
        for i, source in enumerate((held[0], held[1], wide))
    ]
    for fetch in fetches:
        fetch.start()
    for i in range(3):
        fetches[i].wait()
        if i == 2:
            wide[...] = held[2][0 : wide.shape[0], :].astype(jnp.float32)
        stores[i].start()
    for store in stores:
        store.wait()


def on_device(features, mask_packed, neighbours, send_list, weights, cotangent):
    groups, parts = lax.axis_size("space"), lax.axis_size("chan")
    width, bricks = features.shape[0], features.shape[1]
    total = weights.shape[2]
    rows_w = 27 * width
    chunk, owners = plan_chunks(rows_w, groups)
    rows_k = -(-max(rows_w, owners * chunk) // LANES) * LANES
    wide, cube = BRICK * LANES, PLANES * LANES
    scale = 1.0 / math.sqrt(bricks * groups * VOX)
    f32, bf16 = jnp.float32, jnp.bfloat16
    dma = pltpu.SemaphoreType.DMA
    brick_shape = jax.ShapeDtypeStruct((width, bricks, VOX), bf16)
    gw_shape = jax.ShapeDtypeStruct((owners * chunk, total), bf16)
    hbm = pl.BlockSpec(memory_space=pl.ANY)
    results = pl.pallas_call(
        functools.partial(kernel, groups, parts, width, bricks, scale),
        out_shape=(brick_shape, brick_shape, gw_shape),
        in_specs=[hbm] * 6,
        out_specs=(hbm,) * 3,
        scratch_shapes=[
            pltpu.SMEM((bricks, VOX // 32), jnp.int32),
            pltpu.SMEM((bricks, 26), jnp.int32),
            pltpu.SMEM((1, 8), jnp.int32),
            pltpu.VMEM((width, bricks, VOX), bf16),
            pltpu.VMEM((rows_w, total), bf16),
            pltpu.VMEM((width, bricks, VOX), bf16),
            pltpu.VMEM((width, bricks, VOX), bf16),
            pltpu.VMEM((width, bricks, VOX), bf16),
            pltpu.VMEM((owners * chunk, total), bf16),
            dma((6,)), dma((3,)),
            pltpu.VMEM((bricks + 9, TILES, width, LANES), bf16),
            pltpu.VMEM((8, TILES, width, LANES), bf16),
            pltpu.VMEM((9 * LANES, 2 * LANES), bf16),
            pltpu.VMEM((LANES, 2 * LANES), bf16),
            pltpu.VMEM((total, rows_k), bf16),
            pltpu.VMEM((9 * width, 3 * total), bf16),
            pltpu.VMEM((width, bricks * cube), f32),
            pltpu.VMEM((rows_k, bricks * wide), bf16),
            pltpu.VMEM((2, 2, width, bricks * VOX), bf16),
            pltpu.VMEM((2, width, bricks * VOX), bf16),
            pltpu.VMEM((2, width, bricks * VOX), bf16),
            pltpu.VMEM((2, width, bricks * VOX), bf16),
            pltpu.VMEM((2, width, bricks * VOX), bf16),
            pltpu.VMEM((2, 2, width, bricks * VOX), bf16),
            pltpu.VMEM((3 * total, bricks * cube), bf16),
            pltpu.VMEM((9 * width, bricks * cube), f32),
            pltpu.VMEM((8, TILES, width, LANES), bf16),
            pltpu.VMEM((8, TILES, width, LANES), bf16),
            pltpu.VMEM((owners * chunk, total), f32),
            pltpu.VMEM((owners * chunk, total), bf16),
            pltpu.VMEM((groups, chunk, total), bf16),
            dma((8,)), dma((8,)), dma((8,)), dma((8,)),
            dma((bricks,)), dma((bricks,)), dma((bricks,)), dma((bricks,)),
            dma((bricks,)), dma((bricks,)), dma((1,)), dma((1,)),
            dma((groups,)), dma((groups,)), dma((groups,)), dma((groups,)),
        ],
        compiler_params=pltpu.CompilerParams(
            collective_id=0, has_side_effects=True, vmem_limit_bytes=60 * 2**20
        ),
    )(
        mask_packed, neighbours, send_list.reshape(1, 8),
        features, weights.reshape(rows_w, total), cotangent,
    )
    act, grad_feat, grad_w = pl.pallas_call(
        hand_over,
        out_shape=(
            brick_shape, brick_shape, jax.ShapeDtypeStruct((rows_w, total), f32)
        ),
        in_specs=[hbm] * 3,
        out_specs=(hbm,) * 3,
        scratch_shapes=[
            pltpu.VMEM((width, bricks, VOX), bf16),
            pltpu.VMEM((width, bricks, VOX), bf16),
            pltpu.VMEM((owners * chunk, total), bf16),
            pltpu.VMEM((rows_w, total), f32),
            dma((3,)), dma((3,)),
        ],
        compiler_params=pltpu.CompilerParams(vmem_limit_bytes=60 * 2**20),
    )(*results)
    return act, grad_feat, grad_w.reshape(27, width, total)


def solution(mesh):
    return jax.shard_map(
        on_device,
        mesh=mesh,
        in_specs=(
            P("chan", "space", None),
            P("space", None),
            P("space", None),
            P("space", None, None),
            P(None, "chan", None),
            P("chan", "space", None),
        ),
        out_specs=(P("chan", "space", None), P("chan", "space", None), P(None, "chan", None)),
        check_vma=False,
    )
```

```python
import functools
import math

import jax
import jax.numpy as jnp
from jax import lax
from jax.experimental import pallas as pl
from jax.experimental.pallas import tpu as pltpu
from jax.sharding import PartitionSpec as P

BRICK = 8
VOX = 512
LANES = 128
TILES = VOX // LANES
PLANES = BRICK + 2
MESH = pl.DeviceIdType.MESH

tile_moves = [(a, b) for a in (-1, 0, 1) for b in (-1, 0, 1) if (a, b) != (0, 0)]
tile_steps = [a * 4 + b for a, b in tile_moves]
plane_offsets = [(y, z) for y in (-1, 0, 1) for z in (-1, 0, 1)]


def neighbour_slot(along_x, along_y, along_z):
    linear = (along_x + 1) * 9 + (along_y + 1) * 3 + (along_z + 1)
    return linear if linear < 13 else linear - 1


def tile_of(along_x):
    return TILES - 1 if along_x == -1 else 0


def plan_chunks(rows, groups):
    chunk = -(-rows // groups)
    chunk = -(-chunk // 16) * 16
    return chunk, -(-rows // chunk)


def nt_dot(left, right):
    return lax.dot_general(
        left, right, (((1,), (1,)), ((), ())), preferred_element_type=jnp.float32
    )


def nn_dot(left, right):
    return jnp.dot(left, right, preferred_element_type=jnp.float32)


def kernel(
    groups, parts, width, bricks, scale,
    packed_in, near_in, sends_in, feat_in, w_in, cot_in,
    act_out, grad_feat_out, gw_out,
    packed, near, sends, feat, w, cot, act, grad_feat, gw_all, in_s, out_s,
    table, outbox, place, expand, w_turned, w_wide, padded, stacked, comp, mate_in, halves, cross_in, cots, gates,
    window, prod, backbox, back_in, gw_own, gw_send, gw_in,
    halo_s, halo_r, back_s, back_r, mate_s, mate_r, cross_s, cross_r, gate_s, gate_r, cot_s, cot_r, red_s, red_r, all_s, all_r,
):
    me, mine = lax.axis_index("space"), lax.axis_index("chan")
    total = parts * width
    rows_w = 27 * width
    chunk, owners = plan_chunks(rows_w, groups)
    wide = BRICK * LANES
    cube = PLANES * LANES
    f32, bf16 = jnp.float32, jnp.bfloat16

    fetches = [
        pltpu.make_async_copy(source, target, in_s.at[i])
        for i, (source, target) in enumerate(
            (
                (packed_in, packed), (feat_in, feat), (sends_in, sends), (near_in, near),
                (cot_in, cot), (w_in, w),
            )
        )
    ]
    for fetch in fetches:
        fetch.start()
    level, low = mine // 2, lax.rem(mine, 2)
    mate, across = mine + 1 - 2 * low, lax.rem(mine + 2, 4)

    barrier = pltpu.get_barrier_semaphore()
    for d in range(1, groups):
        pl.semaphore_signal(
            barrier, inc=1, device_id=(lax.rem(me + d, groups), mine), device_id_type=MESH
        )
    for peer in (mate, across):
        pl.semaphore_signal(barrier, inc=1, device_id=(me, peer), device_id_type=MESH)

    row = lax.broadcasted_iota(jnp.int32, (LANES, 2 * LANES), 0)
    col = lax.broadcasted_iota(jnp.int32, (LANES, 2 * LANES), 1)
    half, at_y, at_z = row >> 6, (row >> 3) & 7, row & 7
    goal = half * LANES + (at_y + 1) * PLANES + (at_z + 1)
    side_y = {-1: at_y == BRICK - 1, 1: at_y == 0}
    side_z = {-1: at_z == BRICK - 1, 1: at_z == 0}
    for n, (y, z) in enumerate(plane_offsets):
        hit = col == goal + (BRICK * PLANES * y + BRICK * z)
        if y != 0:
            hit = hit & side_y[y]
        if z != 0:
            hit = hit & side_z[z]
        place[n * LANES : (n + 1) * LANES, :] = jnp.where(hit, 1.0, 0.0).astype(bf16)
    expand[...] = jnp.where(col == goal - (PLANES + 1), 1.0, 0.0).astype(bf16)

    for fetch in fetches[:3]:
        fetch.wait()

    lane = lax.broadcasted_iota(jnp.int32, (1, VOX), 1)
    masks = []
    for b in range(bricks):
        word = jnp.zeros((1, VOX), jnp.int32)
        for i in range(VOX // 32):
            word = jnp.where((lane >> 5) == i, packed[b, i], word)
        masks.append((lax.shift_right_logical(word, lane & 31) & 1).astype(f32))

    masked = [
        feat[:, b, :].astype(f32) * masks[b] for b in range(bricks)
    ]
    for b in range(bricks):
        for t in range(TILES):
            table[b, t] = masked[b][:, t * LANES : (t + 1) * LANES].astype(bf16)
    table[bricks + 8] = jnp.zeros((TILES, width, LANES), bf16)
    for k, (a, _) in enumerate(tile_moves):
        chosen = jnp.full((width, LANES), sends[0, k], jnp.int32)
        for t in range(TILES) if a == 0 else (tile_of(a),):
            value = jnp.zeros((width, LANES), f32)
            for b in range(bricks):
                value = jnp.where(chosen == b, masked[b][:, t * LANES : (t + 1) * LANES], value)
            outbox[k, t] = value.astype(bf16)

    pl.semaphore_wait(barrier, groups - 1 + 2)

    tile_a, tile_b = me // 4, lax.rem(me, 4)

    def inside(a, b):
        return (
            (tile_a + a >= 0) & (tile_a + a < groups // 4) & (tile_b + b >= 0) & (tile_b + b < 4)
        )

    def halo(k, box, rows, base, send, recv, sign):
        a, _ = tile_moves[k]
        if a == 0:
            source, target = box.at[k], rows.at[base + k]
        else:
            source, target = box.at[k, tile_of(a)], rows.at[base + k, tile_of(a)]
        peer = jnp.clip(me + sign * tile_steps[k], 0, groups - 1)
        return pltpu.make_async_remote_copy(
            src_ref=source, dst_ref=target, send_sem=send.at[k], recv_sem=recv.at[k],
            device_id=(peer, mine), device_id_type=MESH,
        )

    forth = [halo(k, outbox, table, bricks, halo_s, halo_r, -1) for k in range(8)]
    back = [halo(k, backbox, back_in, 0, back_s, back_r, 1) for k in range(8)]
    ahead = [inside(a, b) for a, b in tile_moves]
    behind = [inside(-a, -b) for a, b in tile_moves]

    def start_if(flag, copy):
        @pl.when(flag)
        def _():
            copy.start()

    def sent_if(flag, copy):
        @pl.when(flag)
        def _():
            copy.wait_send()

    def arrived_if(flag, copy):
        @pl.when(flag)
        def _():
            copy.wait_recv()

    for k in range(8):
        start_if(behind[k], forth[k])

    for fetch in fetches[3:]:
        fetch.wait()
    for b in range(bricks):
        cots[level, :, b * VOX : (b + 1) * VOX] = cot[:, b, :]
    cot_copy = pltpu.make_async_remote_copy(
        src_ref=cots.at[level], dst_ref=cots.at[level], send_sem=cot_s.at[0],
        recv_sem=cot_r.at[0], device_id=(me, across), device_id_type=MESH,
    )
    cot_copy.start()

    rows_k = w_turned.shape[1]
    for c in range(rows_k // LANES):
        have = min(rows_w - c * LANES, LANES)
        block = w[c * LANES : c * LANES + have, :].astype(f32)
        if have < LANES:
            block = jnp.concatenate([block, jnp.zeros((LANES - have, total), f32)], axis=0)
        w_turned[:, c * LANES : (c + 1) * LANES] = block.T.astype(bf16)
    for n in range(9):
        for u in range(3):
            w_wide[n * width : (n + 1) * width, u * total : (u + 1) * total] = w[
                (u * 9 + n) * width : (u * 9 + n + 1) * width, :
            ]
    if rows_k > rows_w:
        stacked[rows_w:, :] = jnp.zeros((rows_k - rows_w, bricks * wide), bf16)
    for u in range(3):
        for b in range(bricks):
            for px in range(PLANES):
                if not u <= px < u + BRICK:
                    window[
                        u * total : (u + 1) * total,
                        b * cube + px * LANES : b * cube + (px + 1) * LANES,
                    ] = jnp.zeros((total, LANES), bf16)

    for k in range(8):
        arrived_if(ahead[k], forth[k])

    columns = []
    for n, (y, z) in enumerate(plane_offsets):
        pieces = []
        for b in range(bricks):
            source = b if (y, z) == (0, 0) else near[b, neighbour_slot(0, y, z)]
            pieces.append(table[source].reshape(TILES * width, LANES))
        for x in (-1, 1):
            for b in range(bricks):
                pieces.append(table[near[b, neighbour_slot(x, y, z)], tile_of(x)])
        columns.append(jnp.concatenate(pieces, axis=0))
    built = nn_dot(jnp.concatenate(columns, axis=1), place[...])
    ends = bricks * TILES * width
    for b in range(bricks):
        base = b * cube
        first = ends + b * width
        last = ends + (bricks + b) * width
        padded[:, base : base + LANES] = built[first : first + width, LANES:]
        padded[:, base + cube - LANES : base + cube] = built[last : last + width, :LANES]
        for t in range(TILES):
            at = (b * TILES + t) * width
            padded[:, base + (2 * t + 1) * LANES : base + (2 * t + 3) * LANES] = built[
                at : at + width, :
            ]

    length = bricks * cube
    shifts = [(y + 1) * PLANES + (z + 1) for y, z in plane_offsets]
    for n in range(9):
        value = padded[...]
        if shifts[n]:
            value = pltpu.roll(value, length - shifts[n], axis=1)
        value = value.astype(bf16)
        for u in range(3):
            for b in range(bricks):
                stacked[
                    (u * 9 + n) * width : (u * 9 + n + 1) * width, b * wide : (b + 1) * wide
                ] = value[:, b * cube + u * LANES : b * cube + u * LANES + wide]

    def chan_copy(source, target, send, recv, peer):
        return pltpu.make_async_remote_copy(
            src_ref=source, dst_ref=target, send_sem=send, recv_sem=recv,
            device_id=(me, peer), device_id_type=MESH,
        )

    spans = [pl.ds(b * VOX, VOX) for b in range(bricks)]
    to_mate = [
        chan_copy(
            comp.at[:, 1 - low, :, spans[b]], mate_in.at[:, :, spans[b]],
            mate_s.at[b], mate_r.at[b], mate,
        )
        for b in range(bricks)
    ]
    to_across = [
        chan_copy(
            halves.at[:, :, spans[b]], cross_in.at[:, :, spans[b]],
            cross_s.at[b], cross_r.at[b], across,
        )
        for b in range(bricks)
    ]
    to_both = [
        chan_copy(
            gates.at[:, low, :, spans[b]], gates.at[:, low, :, spans[b]],
            gate_s.at[b], gate_r.at[b], mate,
        )
        for b in range(bricks)
    ]

    for b in range(bricks):
        for t in range(TILES):
            i = b * TILES + t
            part = nn_dot(w_turned[...], stacked[:, 2 * i * LANES : 2 * (i + 1) * LANES])
            comp[:, :, :, i * LANES : (i + 1) * LANES] = (
                nt_dot(part.astype(bf16), expand[...])
                .astype(bf16)
                .reshape(2, 2, width, LANES)
            )
        to_mate[b].start()

    for b in range(bricks):
        to_mate[b].wait_recv()
        halves[:, :, spans[b]] = (
            comp[:, low, :, spans[b]].astype(f32) + mate_in[:, :, spans[b]].astype(f32)
        ).astype(bf16)
        to_across[b].start()

    cot_copy.wait_recv()
    for b in range(bricks):
        to_across[b].wait_recv()
        for h in range(2):
            pre = halves[h, :, spans[b]].astype(f32) + cross_in[h, :, spans[b]].astype(f32)
            pre = pre * masks[b]
            gate = jax.nn.sigmoid(pre)
            gates[h, low, :, spans[b]] = (
                cots[h, :, spans[b]].astype(f32) * masks[b] * gate * (1.0 + pre * (1.0 - gate))
            ).astype(bf16)

        to_both[b].start()
    for b in range(bricks):
        pre = halves[level, :, spans[b]].astype(f32) + cross_in[level, :, spans[b]].astype(f32)
        pre = pre * masks[b]
        act[:, b, :] = (pre * jax.nn.sigmoid(pre)).astype(bf16)
    act_copy = pltpu.make_async_copy(act, act_out, out_s.at[0])
    act_copy.start()

    for b in range(bricks):
        to_both[b].wait_recv()
        for t in range(TILES):
            i = b * TILES + t
            value = gates[:, :, :, i * LANES : (i + 1) * LANES].reshape(total, LANES)
            value = nn_dot(value, expand[...]).astype(bf16)
            for u in range(3):
                at = b * cube + (u + 2 * t) * LANES
                window[u * total : (u + 1) * total, at : at + 2 * LANES] = value

    def chunk_rows(index):
        return pl.ds(pl.multiple_of(index * chunk, 16), chunk)

    def reduce_copy(d):
        peer = lax.rem(me + d, groups)
        kept = jnp.minimum(peer, owners - 1)
        return peer, pltpu.make_async_remote_copy(
            src_ref=gw_send.at[chunk_rows(kept)], dst_ref=gw_in.at[d],
            send_sem=red_s.at[d], recv_sem=red_r.at[d],
            device_id=(peer, mine), device_id_type=MESH,
        )

    kept_me = jnp.minimum(me, owners - 1)

    partner = me + 1 - 2 * lax.rem(me, 2)
    pairs = groups // 2

    def share_copy(k):
        span = gw_all.at[chunk_rows(kept_me)]
        peer = partner if k == 0 else lax.rem(me + 2 * k, groups)
        return pltpu.make_async_remote_copy(
            src_ref=span, dst_ref=span, send_sem=all_s.at[k], recv_sem=all_r.at[k],
            device_id=(peer, mine), device_id_type=MESH,
        )

    def source_of(device, k):
        return lax.rem(device + groups - 2 * k, groups)

    def forward_copy(k):
        span = gw_all.at[chunk_rows(jnp.minimum(source_of(me, k), owners - 1))]
        return pltpu.make_async_remote_copy(
            src_ref=span, dst_ref=span, send_sem=all_s.at[pairs + k],
            recv_sem=all_r.at[pairs + k], device_id=(partner, mine), device_id_type=MESH,
        )

    def guarded(flag, action):
        if owners == groups:
            action()
        else:
            pl.when(flag)(action)

    pack = 2 if owners % 2 == 0 else 1
    packs = owners // pack
    for i in range(packs):
        first = lax.rem(me // pack + i + 1, packs) * pack
        span = pl.ds(pl.multiple_of(first * chunk, 16), pack * chunk)
        value = None
        for b in range(bricks):
            term = nt_dot(
                stacked[span, b * wide : (b + 1) * wide],
                window[total : 2 * total, b * cube + LANES : b * cube + LANES + wide],
            )
            value = term if value is None else value + term
        gw_own[span, :] = value
        gw_send[span, :] = value.astype(bf16)
        for c in range(pack):
            copy = reduce_copy(lax.rem(first + c - me + groups, groups))[1]
            if groups == owners and i < packs - 1:
                copy.start()
            else:
                pl.when(first + c != me)(copy.start)

    for i in range(length // (2 * LANES)):
        span = slice(2 * i * LANES, 2 * (i + 1) * LANES)
        prod[:, span] = nn_dot(w_wide[...], window[:, span])
    spread = prod[0:width, :]
    for n in range(1, 9):
        spread = spread + pltpu.roll(prod[n * width : (n + 1) * width, :], shifts[n], axis=1)
    padded[...] = spread

    def add_up():
        value = gw_own[chunk_rows(kept_me), :]
        for d in range(1, groups):
            reduce_copy(d)[1].wait_recv()
            value = value + gw_in[d].astype(f32)
        gw_all[chunk_rows(kept_me), :] = (value * scale).astype(bf16)
        for k in range(pairs):
            share_copy((k + 1) % pairs).start()

    guarded(me < owners, add_up)

    pieces = []
    blank = jnp.zeros((width, LANES), f32)
    for b in range(bricks):
        for t in range(TILES):
            at = b * cube + (2 * t + 1) * LANES
            pieces.append(padded[:, at : at + 2 * LANES])
    for b in range(bricks):
        pieces.append(jnp.concatenate([blank, padded[:, b * cube : b * cube + LANES]], axis=1))
    for b in range(bricks):
        at = (b + 1) * cube - LANES
        pieces.append(jnp.concatenate([padded[:, at : at + LANES], blank], axis=1))
    rims = jnp.concatenate(pieces, axis=0).astype(bf16)

    whole = TILES * width
    own = [jnp.zeros((whole, LANES), f32) for _ in range(bricks)]
    own_end = {(b, x): blank for b in range(bricks) for x in (-1, 1)}
    slots = [jnp.zeros((whole if a == 0 else width, LANES), f32) for a, _ in tile_moves]

    def picked(index, wanted, value):
        return jnp.where(jnp.full(value.shape, index, jnp.int32) == wanted, value, 0.0)

    for n, (y, z) in enumerate(plane_offsets):
        folded = nt_dot(rims, place[n * LANES : (n + 1) * LANES, :])
        for x in (-1, 0, 1):
            slot = None if (x, y) == (0, 0) else tile_moves.index((x, y))
            for b in range(bricks):
                if x == 0:
                    piece = folded[b * whole : (b + 1) * whole]
                else:
                    at = ends + (b if x == -1 else bricks + b) * width
                    piece = folded[at : at + width]
                if (x, y, z) == (0, 0, 0):
                    own[b] = own[b] + piece
                    continue
                index = near[b, neighbour_slot(x, y, z)]
                for c in range(bricks):
                    term = picked(index, c, piece)
                    if x == 0:
                        own[c] = own[c] + term
                    else:
                        own_end[c, x] = own_end[c, x] + term
                if slot is not None:
                    slots[slot] = slots[slot] + picked(index, bricks + slot, piece)
    for k, (a, _) in enumerate(tile_moves):
        if a == 0:
            backbox[k] = slots[k].astype(bf16).reshape(TILES, width, LANES)
        else:
            backbox[k, tile_of(a)] = slots[k].astype(bf16)
        start_if(ahead[k], back[k])

    for k in range(1, pairs):
        flag = source_of(me, k) < owners
        guarded(flag, share_copy(k).wait_recv)
        guarded(flag, forward_copy(k).start)

    for k in range(8):
        arrived_if(behind[k], back[k])
    for b in range(bricks):
        rows = []
        for t in range(TILES):
            value = own[b][t * width : (t + 1) * width]
            for x in (-1, 1):
                if t == tile_of(x):
                    value = value + own_end[b, x]
            for k, (a, _) in enumerate(tile_moves):
                if a == 0 or t == tile_of(a):
                    value = value + picked(sends[0, k], b, back_in[k, t].astype(f32))
            rows.append((value * masks[b][:, t * LANES : (t + 1) * LANES]).astype(bf16))
        grad_feat[:, b, :] = jnp.concatenate(rows, axis=1)
    feat_copy = pltpu.make_async_copy(grad_feat, grad_feat_out, out_s.at[1])
    feat_copy.start()

    guarded(partner < owners, share_copy(0).wait_recv)
    for k in range(1, pairs):
        guarded(source_of(partner, k) < owners, forward_copy(k).wait_recv)
    gw_copy = pltpu.make_async_copy(gw_all, gw_out, out_s.at[2])
    gw_copy.start()

    for k in range(8):
        sent_if(behind[k], forth[k])
        sent_if(ahead[k], back[k])
    for b in range(bricks):
        to_mate[b].wait_send()
        to_across[b].wait_send()
        to_both[b].wait_send()
    cot_copy.wait_send()
    for d in range(1, groups):
        peer, copy = reduce_copy(d)
        guarded(peer < owners, copy.wait_send)
    for k in range(pairs):
        guarded(me < owners, share_copy(k).wait_send)
        if k:
            guarded(source_of(me, k) < owners, forward_copy(k).wait_send)
    act_copy.wait()
    feat_copy.wait()
    gw_copy.wait()


def hand_over(*refs):
    sources, targets, held, wide, in_s, out_s = refs[:3], refs[3:6], refs[6:9], refs[9], *refs[10:]
    fetches = [pltpu.make_async_copy(sources[i], held[i], in_s.at[i]) for i in range(3)]
    stores = [
        pltpu.make_async_copy(source, targets[i], out_s.at[i])
        for i, source in enumerate((held[0], held[1], wide))
    ]
    for fetch in fetches:
        fetch.start()
    for i in range(3):
        fetches[i].wait()
        if i == 2:
            wide[...] = held[2][0 : wide.shape[0], :].astype(jnp.float32)
        stores[i].start()
    for store in stores:
        store.wait()


def on_device(features, mask_packed, neighbours, send_list, weights, cotangent):
    groups, parts = lax.axis_size("space"), lax.axis_size("chan")
    width, bricks = features.shape[0], features.shape[1]
    total = weights.shape[2]
    rows_w = 27 * width
    chunk, owners = plan_chunks(rows_w, groups)
    rows_k = -(-max(rows_w, owners * chunk) // LANES) * LANES
    wide, cube = BRICK * LANES, PLANES * LANES
    scale = 1.0 / math.sqrt(bricks * groups * VOX)
    f32, bf16 = jnp.float32, jnp.bfloat16
    dma = pltpu.SemaphoreType.DMA
    brick_shape = jax.ShapeDtypeStruct((width, bricks, VOX), bf16)
    gw_shape = jax.ShapeDtypeStruct((owners * chunk, total), bf16)
    hbm = pl.BlockSpec(memory_space=pl.ANY)
    results = pl.pallas_call(
        functools.partial(kernel, groups, parts, width, bricks, scale),
        out_shape=(brick_shape, brick_shape, gw_shape),
        in_specs=[hbm] * 6,
        out_specs=(hbm,) * 3,
        scratch_shapes=[
            pltpu.SMEM((bricks, VOX // 32), jnp.int32),
            pltpu.SMEM((bricks, 26), jnp.int32),
            pltpu.SMEM((1, 8), jnp.int32),
            pltpu.VMEM((width, bricks, VOX), bf16),
            pltpu.VMEM((rows_w, total), bf16),
            pltpu.VMEM((width, bricks, VOX), bf16),
            pltpu.VMEM((width, bricks, VOX), bf16),
            pltpu.VMEM((width, bricks, VOX), bf16),
            pltpu.VMEM((owners * chunk, total), bf16),
            dma((6,)), dma((3,)),
            pltpu.VMEM((bricks + 9, TILES, width, LANES), bf16),
            pltpu.VMEM((8, TILES, width, LANES), bf16),
            pltpu.VMEM((9 * LANES, 2 * LANES), bf16),
            pltpu.VMEM((LANES, 2 * LANES), bf16),
            pltpu.VMEM((total, rows_k), bf16),
            pltpu.VMEM((9 * width, 3 * total), bf16),
            pltpu.VMEM((width, bricks * cube), f32),
            pltpu.VMEM((rows_k, bricks * wide), bf16),
            pltpu.VMEM((2, 2, width, bricks * VOX), bf16),
            pltpu.VMEM((2, width, bricks * VOX), bf16),
            pltpu.VMEM((2, width, bricks * VOX), bf16),
            pltpu.VMEM((2, width, bricks * VOX), bf16),
            pltpu.VMEM((2, width, bricks * VOX), bf16),
            pltpu.VMEM((2, 2, width, bricks * VOX), bf16),
            pltpu.VMEM((3 * total, bricks * cube), bf16),
            pltpu.VMEM((9 * width, bricks * cube), f32),
            pltpu.VMEM((8, TILES, width, LANES), bf16),
            pltpu.VMEM((8, TILES, width, LANES), bf16),
            pltpu.VMEM((owners * chunk, total), f32),
            pltpu.VMEM((owners * chunk, total), bf16),
            pltpu.VMEM((groups, chunk, total), bf16),
            dma((8,)), dma((8,)), dma((8,)), dma((8,)),
            dma((bricks,)), dma((bricks,)), dma((bricks,)), dma((bricks,)),
            dma((bricks,)), dma((bricks,)), dma((1,)), dma((1,)),
            dma((groups,)), dma((groups,)), dma((groups,)), dma((groups,)),
        ],
        compiler_params=pltpu.CompilerParams(
            collective_id=0, has_side_effects=True, vmem_limit_bytes=60 * 2**20
        ),
    )(
        mask_packed, neighbours, send_list.reshape(1, 8),
        features, weights.reshape(rows_w, total), cotangent,
    )
    act, grad_feat, grad_w = pl.pallas_call(
        hand_over,
        out_shape=(
            brick_shape, brick_shape, jax.ShapeDtypeStruct((rows_w, total), f32)
        ),
        in_specs=[hbm] * 3,
        out_specs=(hbm,) * 3,
        scratch_shapes=[
            pltpu.VMEM((width, bricks, VOX), bf16),
            pltpu.VMEM((width, bricks, VOX), bf16),
            pltpu.VMEM((owners * chunk, total), bf16),
            pltpu.VMEM((rows_w, total), f32),
            dma((3,)), dma((3,)),
        ],
        compiler_params=pltpu.CompilerParams(vmem_limit_bytes=60 * 2**20),
    )(*results)
    return act, grad_feat, grad_w.reshape(27, width, total)


def solution(mesh):
    return jax.shard_map(
        on_device,
        mesh=mesh,
        in_specs=(
            P("chan", "space", None),
            P("space", None),
            P("space", None),
            P("space", None, None),
            P(None, "chan", None),
            P("chan", "space", None),
        ),
        out_specs=(P("chan", "space", None), P("chan", "space", None), P(None, "chan", None)),
        check_vma=False,
    )
```

```python
import functools
import math

import jax
import jax.numpy as jnp
from jax import lax
from jax.experimental import pallas as pl
from jax.experimental.pallas import tpu as pltpu
from jax.sharding import PartitionSpec as P

BRICK = 8
VOX = 512
LANES = 128
TILES = VOX // LANES
PLANES = BRICK + 2
MESH = pl.DeviceIdType.MESH

tile_moves = [(a, b) for a in (-1, 0, 1) for b in (-1, 0, 1) if (a, b) != (0, 0)]
tile_steps = [a * 4 + b for a, b in tile_moves]
plane_offsets = [(y, z) for y in (-1, 0, 1) for z in (-1, 0, 1)]


def neighbour_slot(along_x, along_y, along_z):
    linear = (along_x + 1) * 9 + (along_y + 1) * 3 + (along_z + 1)
    return linear if linear < 13 else linear - 1


def tile_of(along_x):
    return TILES - 1 if along_x == -1 else 0


def plan_chunks(rows, groups):
    chunk = -(-rows // groups)
    chunk = -(-chunk // 16) * 16
    return chunk, -(-rows // chunk)


def nt_dot(left, right):
    return lax.dot_general(
        left, right, (((1,), (1,)), ((), ())), preferred_element_type=jnp.float32
    )


def nn_dot(left, right):
    return jnp.dot(left, right, preferred_element_type=jnp.float32)


def kernel(
    groups, parts, width, bricks, scale,
    packed_in, near_in, sends_in, feat_in, w_in, cot_in,
    act_out, grad_feat_out, gw_out,
    packed, near, sends, feat, w, cot, act, grad_feat, gw_all, in_s, out_s,
    table, outbox, place, expand, fold, compact, rimmed, w_turned, w_wide, padded, stacked, comp, mate_in, halves, cross_in, cots, gates,
    window, prod, backbox, back_in, gw_own, gw_send, gw_in,
    halo_s, halo_r, back_s, back_r, mate_s, mate_r, cross_s, cross_r, gate_s, gate_r, cot_s, cot_r, red_s, red_r, all_s, all_r,
):
    me, mine = lax.axis_index("space"), lax.axis_index("chan")
    total = parts * width
    rows_w = 27 * width
    chunk, owners = plan_chunks(rows_w, groups)
    wide = BRICK * LANES
    cube = PLANES * LANES
    f32, bf16 = jnp.float32, jnp.bfloat16

    fetches = [
        pltpu.make_async_copy(source, target, in_s.at[i])
        for i, (source, target) in enumerate(
            (
                (packed_in, packed), (feat_in, feat), (sends_in, sends), (near_in, near),
                (cot_in, cot), (w_in, w),
            )
        )
    ]
    for fetch in fetches:
        fetch.start()
    level, low = mine // 2, lax.rem(mine, 2)
    mate, across = mine + 1 - 2 * low, lax.rem(mine + 2, 4)

    barrier = pltpu.get_barrier_semaphore()
    for d in range(1, groups):
        pl.semaphore_signal(
            barrier, inc=1, device_id=(lax.rem(me + d, groups), mine), device_id_type=MESH
        )
    for peer in (mate, across):
        pl.semaphore_signal(barrier, inc=1, device_id=(me, peer), device_id_type=MESH)

    row = lax.broadcasted_iota(jnp.int32, (LANES, 2 * LANES), 0)
    col = lax.broadcasted_iota(jnp.int32, (LANES, 2 * LANES), 1)
    half, at_y, at_z = row >> 6, (row >> 3) & 7, row & 7
    goal = half * LANES + (at_y + 1) * PLANES + (at_z + 1)
    side_y = {-1: at_y == BRICK - 1, 1: at_y == 0}
    side_z = {-1: at_z == BRICK - 1, 1: at_z == 0}
    for n, (y, z) in enumerate(plane_offsets):
        hit = col == goal + (BRICK * PLANES * y + BRICK * z)
        if y != 0:
            hit = hit & side_y[y]
        if z != 0:
            hit = hit & side_z[z]
        place[n * LANES : (n + 1) * LANES, :] = jnp.where(hit, 1.0, 0.0).astype(bf16)
    row_t = lax.broadcasted_iota(jnp.int32, (2 * LANES, LANES), 0)
    col_t = lax.broadcasted_iota(jnp.int32, (2 * LANES, LANES), 1)
    goal_t = (col_t >> 6) * LANES + (((col_t >> 3) & 7) + 1) * PLANES + ((col_t & 7) + 1)
    compact[...] = jnp.where(row_t == goal_t - (PLANES + 1), 1.0, 0.0).astype(bf16)
    expand[...] = jnp.where(col == goal - (PLANES + 1), 1.0, 0.0).astype(bf16)

    for fetch in fetches[:3]:
        fetch.wait()

    lane = lax.broadcasted_iota(jnp.int32, (1, VOX), 1)
    masks = []
    for b in range(bricks):
        word = jnp.zeros((1, VOX), jnp.int32)
        for i in range(VOX // 32):
            word = jnp.where((lane >> 5) == i, packed[b, i], word)
        masks.append((lax.shift_right_logical(word, lane & 31) & 1).astype(f32))

    masked = [
        feat[:, b, :].astype(f32) * masks[b] for b in range(bricks)
    ]
    for b in range(bricks):
        for t in range(TILES):
            table[b, t] = masked[b][:, t * LANES : (t + 1) * LANES].astype(bf16)
    table[bricks + 8] = jnp.zeros((TILES, width, LANES), bf16)
    for k, (a, _) in enumerate(tile_moves):
        chosen = jnp.full((width, LANES), sends[0, k], jnp.int32)
        for t in range(TILES) if a == 0 else (tile_of(a),):
            value = jnp.zeros((width, LANES), f32)
            for b in range(bricks):
                value = jnp.where(chosen == b, masked[b][:, t * LANES : (t + 1) * LANES], value)
            outbox[k, t] = value.astype(bf16)

    pl.semaphore_wait(barrier, groups - 1 + 2)

    tile_a, tile_b = me // 4, lax.rem(me, 4)

    def inside(a, b):
        return (
            (tile_a + a >= 0) & (tile_a + a < groups // 4) & (tile_b + b >= 0) & (tile_b + b < 4)
        )

    def halo(k, box, rows, base, send, recv, sign):
        a, _ = tile_moves[k]
        if a == 0:
            source, target = box.at[k], rows.at[base + k]
        else:
            source, target = box.at[k, tile_of(a)], rows.at[base + k, tile_of(a)]
        peer = jnp.clip(me + sign * tile_steps[k], 0, groups - 1)
        return pltpu.make_async_remote_copy(
            src_ref=source, dst_ref=target, send_sem=send.at[k], recv_sem=recv.at[k],
            device_id=(peer, mine), device_id_type=MESH,
        )

    forth = [halo(k, outbox, table, bricks, halo_s, halo_r, -1) for k in range(8)]
    back = [halo(k, backbox, back_in, 0, back_s, back_r, 1) for k in range(8)]
    ahead = [inside(a, b) for a, b in tile_moves]
    behind = [inside(-a, -b) for a, b in tile_moves]

    def start_if(flag, copy):
        @pl.when(flag)
        def _():
            copy.start()

    def sent_if(flag, copy):
        @pl.when(flag)
        def _():
            copy.wait_send()

    def arrived_if(flag, copy):
        @pl.when(flag)
        def _():
            copy.wait_recv()

    for k in range(8):
        start_if(behind[k], forth[k])

    for fetch in fetches[3:]:
        fetch.wait()
    for b in range(bricks):
        cots[level, :, b * VOX : (b + 1) * VOX] = cot[:, b, :]
    cot_copy = pltpu.make_async_remote_copy(
        src_ref=cots.at[level], dst_ref=cots.at[level], send_sem=cot_s.at[0],
        recv_sem=cot_r.at[0], device_id=(me, across), device_id_type=MESH,
    )
    cot_copy.start()

    rows_k = w_turned.shape[1]
    for c in range(rows_k // LANES):
        have = min(rows_w - c * LANES, LANES)
        block = w[c * LANES : c * LANES + have, :].astype(f32)
        if have < LANES:
            block = jnp.concatenate([block, jnp.zeros((LANES - have, total), f32)], axis=0)
        w_turned[:, c * LANES : (c + 1) * LANES] = block.T.astype(bf16)
    if rows_k > rows_w:
        stacked[rows_w:, :] = jnp.zeros((rows_k - rows_w, bricks * wide), bf16)
    for k in range(8):
        arrived_if(ahead[k], forth[k])

    columns = []
    for n, (y, z) in enumerate(plane_offsets):
        pieces = []
        for b in range(bricks):
            source = b if (y, z) == (0, 0) else near[b, neighbour_slot(0, y, z)]
            pieces.append(table[source].reshape(TILES * width, LANES))
        for x in (-1, 1):
            for b in range(bricks):
                pieces.append(table[near[b, neighbour_slot(x, y, z)], tile_of(x)])
        columns.append(jnp.concatenate(pieces, axis=0))
    built = nn_dot(jnp.concatenate(columns, axis=1), place[...]).astype(bf16)
    ends = bricks * TILES * width
    for b in range(bricks):
        base = b * cube
        first = ends + b * width
        last = ends + (bricks + b) * width
        rimmed[:, base : base + LANES] = built[first : first + width, LANES:]
        rimmed[:, base + cube - LANES : base + cube] = built[last : last + width, :LANES]
        for t in range(TILES):
            at = (b * TILES + t) * width
            rimmed[:, base + (2 * t + 1) * LANES : base + (2 * t + 3) * LANES] = built[
                at : at + width, :
            ]

    length = bricks * cube
    shifts = [(y + 1) * PLANES + (z + 1) for y, z in plane_offsets]
    for n in range(9):
        value = rimmed[...]
        if shifts[n]:
            value = pltpu.roll(value, length - shifts[n], axis=1)
        for u in range(3):
            for b in range(bricks):
                stacked[
                    (u * 9 + n) * width : (u * 9 + n + 1) * width, b * wide : (b + 1) * wide
                ] = value[:, b * cube + u * LANES : b * cube + u * LANES + wide]

    def chan_copy(source, target, send, recv, peer):
        return pltpu.make_async_remote_copy(
            src_ref=source, dst_ref=target, send_sem=send, recv_sem=recv,
            device_id=(me, peer), device_id_type=MESH,
        )

    spans = [pl.ds(b * VOX, VOX) for b in range(bricks)]
    to_mate = [
        chan_copy(
            comp.at[:, 1 - low, :, spans[b]], mate_in.at[:, :, spans[b]],
            mate_s.at[b], mate_r.at[b], mate,
        )
        for b in range(bricks)
    ]
    to_across = [
        chan_copy(
            halves.at[:, :, spans[b]], cross_in.at[:, :, spans[b]],
            cross_s.at[b], cross_r.at[b], across,
        )
        for b in range(bricks)
    ]
    to_both = [
        chan_copy(
            gates.at[:, low, :, spans[b]], gates.at[:, low, :, spans[b]],
            gate_s.at[b], gate_r.at[b], mate,
        )
        for b in range(bricks)
    ]

    for b in range(bricks):
        for t in range(TILES):
            i = b * TILES + t
            part = nn_dot(w_turned[...], stacked[:, 2 * i * LANES : 2 * (i + 1) * LANES])
            comp[:, :, :, i * LANES : (i + 1) * LANES] = (
                nn_dot(part.astype(bf16), compact[...])
                .astype(bf16)
                .reshape(2, 2, width, LANES)
            )
        to_mate[b].start()

    for b in range(bricks):
        to_mate[b].wait_recv()
        halves[:, :, spans[b]] = (
            comp[:, low, :, spans[b]].astype(f32) + mate_in[:, :, spans[b]].astype(f32)
        ).astype(bf16)
        to_across[b].start()

    for n in range(9):
        for u in range(3):
            w_wide[n * width : (n + 1) * width, u * total : (u + 1) * total] = w[
                (u * 9 + n) * width : (u * 9 + n + 1) * width, :
            ]
    for u in range(3):
        for b in range(bricks):
            for px in range(PLANES):
                if not u <= px < u + BRICK:
                    window[
                        u * total : (u + 1) * total,
                        b * cube + px * LANES : b * cube + (px + 1) * LANES,
                    ] = jnp.zeros((total, LANES), bf16)

    for n, (y, z) in enumerate(plane_offsets):
        hit = row_t == goal_t + (BRICK * PLANES * y + BRICK * z)
        if y != 0:
            hit = hit & ((col_t >> 3) & 7 == (BRICK - 1 if y == -1 else 0))
        if z != 0:
            hit = hit & (col_t & 7 == (BRICK - 1 if z == -1 else 0))
        fold[:, n * LANES : (n + 1) * LANES] = jnp.where(hit, 1.0, 0.0).astype(bf16)

    cot_copy.wait_recv()
    for b in range(bricks):
        to_across[b].wait_recv()
        for h in range(2):
            pre = halves[h, :, spans[b]].astype(f32) + cross_in[h, :, spans[b]].astype(f32)
            pre = pre * masks[b]
            gate = jax.nn.sigmoid(pre)
            gates[h, low, :, spans[b]] = (
                cots[h, :, spans[b]].astype(f32) * masks[b] * gate * (1.0 + pre * (1.0 - gate))
            ).astype(bf16)

        to_both[b].start()
    for b in range(bricks):
        pre = halves[level, :, spans[b]].astype(f32) + cross_in[level, :, spans[b]].astype(f32)
        pre = pre * masks[b]
        act[:, b, :] = (pre * jax.nn.sigmoid(pre)).astype(bf16)
    act_copy = pltpu.make_async_copy(act, act_out, out_s.at[0])
    act_copy.start()

    for b in range(bricks):
        to_both[b].wait_recv()
        for t in range(TILES):
            i = b * TILES + t
            value = gates[:, :, :, i * LANES : (i + 1) * LANES].reshape(total, LANES)
            value = nn_dot(value, expand[...]).astype(bf16)
            for u in range(3):
                at = b * cube + (u + 2 * t) * LANES
                window[u * total : (u + 1) * total, at : at + 2 * LANES] = value

    def chunk_rows(index):
        return pl.ds(pl.multiple_of(index * chunk, 16), chunk)

    def reduce_copy(d):
        peer = lax.rem(me + d, groups)
        kept = jnp.minimum(peer, owners - 1)
        return peer, pltpu.make_async_remote_copy(
            src_ref=gw_send.at[chunk_rows(kept)], dst_ref=gw_in.at[d],
            send_sem=red_s.at[d], recv_sem=red_r.at[d],
            device_id=(peer, mine), device_id_type=MESH,
        )

    kept_me = jnp.minimum(me, owners - 1)

    def share_copy(d):
        peer = lax.rem(me + d, groups)
        span = gw_all.at[chunk_rows(kept_me)]
        return pltpu.make_async_remote_copy(
            src_ref=span, dst_ref=span, send_sem=all_s.at[d], recv_sem=all_r.at[d],
            device_id=(peer, mine), device_id_type=MESH,
        )

    def guarded(flag, action):
        if owners == groups:
            action()
        else:
            pl.when(flag)(action)

    pack = 2 if owners % 2 == 0 else 1
    packs = owners // pack
    for i in range(packs):
        first = lax.rem(me // pack + i + 1, packs) * pack
        span = pl.ds(pl.multiple_of(first * chunk, 16), pack * chunk)
        value = None
        for b in range(bricks):
            term = nt_dot(
                stacked[span, b * wide : (b + 1) * wide],
                window[total : 2 * total, b * cube + LANES : b * cube + LANES + wide],
            )
            value = term if value is None else value + term
        gw_own[span, :] = value
        gw_send[span, :] = value.astype(bf16)
        for c in range(pack):
            copy = reduce_copy(lax.rem(first + c - me + groups, groups))[1]
            if groups == owners and i < packs - 1:
                copy.start()
            else:
                pl.when(first + c != me)(copy.start)

    for i in range(length // (2 * LANES)):
        span = slice(2 * i * LANES, 2 * (i + 1) * LANES)
        prod[:, span] = nn_dot(w_wide[...], window[:, span])
    spread = prod[0:width, :]
    for n in range(1, 9):
        spread = spread + pltpu.roll(prod[n * width : (n + 1) * width, :], shifts[n], axis=1)
    padded[...] = spread

    pieces = []
    blank = jnp.zeros((width, LANES), f32)
    for b in range(bricks):
        for t in range(TILES):
            at = b * cube + (2 * t + 1) * LANES
            pieces.append(padded[:, at : at + 2 * LANES])
    for b in range(bricks):
        pieces.append(jnp.concatenate([blank, padded[:, b * cube : b * cube + LANES]], axis=1))
    for b in range(bricks):
        at = (b + 1) * cube - LANES
        pieces.append(jnp.concatenate([padded[:, at : at + LANES], blank], axis=1))
    rims = jnp.concatenate(pieces, axis=0).astype(bf16)

    whole = TILES * width
    own = [jnp.zeros((whole, LANES), f32) for _ in range(bricks)]
    own_end = {(b, x): blank for b in range(bricks) for x in (-1, 1)}
    slots = [jnp.zeros((whole if a == 0 else width, LANES), f32) for a, _ in tile_moves]

    def weighed(index, wanted, value):
        return value * jnp.where(index == wanted, 1.0, 0.0).astype(f32)

    def picked(index, wanted, value):
        return jnp.where(jnp.full(value.shape, index, jnp.int32) == wanted, value, 0.0)

    for n, (y, z) in enumerate(plane_offsets):
        folded = nn_dot(rims, fold[:, n * LANES : (n + 1) * LANES])
        for x in (-1, 0, 1):
            slot = None if (x, y) == (0, 0) else tile_moves.index((x, y))
            for b in range(bricks):
                if x == 0:
                    piece = folded[b * whole : (b + 1) * whole]
                else:
                    at = ends + (b if x == -1 else bricks + b) * width
                    piece = folded[at : at + width]
                if (x, y, z) == (0, 0, 0):
                    own[b] = own[b] + piece
                    continue
                index = near[b, neighbour_slot(x, y, z)]
                for c in range(bricks):
                    term = weighed(index, c, piece)
                    if x == 0:
                        own[c] = own[c] + term
                    else:
                        own_end[c, x] = own_end[c, x] + term
                if slot is not None:
                    slots[slot] = slots[slot] + weighed(index, bricks + slot, piece)
    for k, (a, _) in enumerate(tile_moves):
        if a == 0:
            backbox[k] = slots[k].astype(bf16).reshape(TILES, width, LANES)
        else:
            backbox[k, tile_of(a)] = slots[k].astype(bf16)
        start_if(ahead[k], back[k])

    def add_up():
        value = gw_own[chunk_rows(kept_me), :]
        for d in range(1, groups):
            reduce_copy(d)[1].wait_recv()
            value = value + gw_in[d].astype(f32)
        gw_all[chunk_rows(kept_me), :] = (value * scale).astype(bf16)
        for d in range(1, groups):
            share_copy(d).start()

    guarded(me < owners, add_up)

    for k in range(8):
        arrived_if(behind[k], back[k])
    for b in range(bricks):
        rows = []
        for t in range(TILES):
            value = own[b][t * width : (t + 1) * width]
            for x in (-1, 1):
                if t == tile_of(x):
                    value = value + own_end[b, x]
            for k, (a, _) in enumerate(tile_moves):
                if a == 0 or t == tile_of(a):
                    value = value + picked(sends[0, k], b, back_in[k, t].astype(f32))
            rows.append((value * masks[b][:, t * LANES : (t + 1) * LANES]).astype(bf16))
        grad_feat[:, b, :] = jnp.concatenate(rows, axis=1)
    feat_copy = pltpu.make_async_copy(grad_feat, grad_feat_out, out_s.at[1])
    feat_copy.start()

    for d in range(1, groups):
        source = lax.rem(me + groups - d, groups)
        guarded(source < owners, share_copy(d).wait_recv)
    gw_copy = pltpu.make_async_copy(gw_all, gw_out, out_s.at[2])
    gw_copy.start()

    for k in range(8):
        sent_if(behind[k], forth[k])
        sent_if(ahead[k], back[k])
    for b in range(bricks):
        to_mate[b].wait_send()
        to_across[b].wait_send()
        to_both[b].wait_send()
    cot_copy.wait_send()
    for d in range(1, groups):
        peer, copy = reduce_copy(d)
        guarded(peer < owners, copy.wait_send)
        guarded(me < owners, share_copy(d).wait_send)
    act_copy.wait()
    feat_copy.wait()
    gw_copy.wait()


def hand_over(*refs):
    sources, targets, held, wide, in_s, out_s = refs[:3], refs[3:6], refs[6:9], refs[9], *refs[10:]
    fetches = [pltpu.make_async_copy(sources[i], held[i], in_s.at[i]) for i in range(3)]
    stores = [
        pltpu.make_async_copy(source, targets[i], out_s.at[i])
        for i, source in enumerate((held[0], held[1], wide))
    ]
    for fetch in fetches:
        fetch.start()
    for i in range(3):
        fetches[i].wait()
        if i == 2:
            wide[...] = held[2][0 : wide.shape[0], :].astype(jnp.float32)
        stores[i].start()
    for store in stores:
        store.wait()


def on_device(features, mask_packed, neighbours, send_list, weights, cotangent):
    groups, parts = lax.axis_size("space"), lax.axis_size("chan")
    width, bricks = features.shape[0], features.shape[1]
    total = weights.shape[2]
    rows_w = 27 * width
    chunk, owners = plan_chunks(rows_w, groups)
    rows_k = -(-max(rows_w, owners * chunk) // LANES) * LANES
    wide, cube = BRICK * LANES, PLANES * LANES
    scale = 1.0 / math.sqrt(bricks * groups * VOX)
    f32, bf16 = jnp.float32, jnp.bfloat16
    dma = pltpu.SemaphoreType.DMA
    brick_shape = jax.ShapeDtypeStruct((width, bricks, VOX), bf16)
    gw_shape = jax.ShapeDtypeStruct((owners * chunk, total), bf16)
    hbm = pl.BlockSpec(memory_space=pl.ANY)
    results = pl.pallas_call(
        functools.partial(kernel, groups, parts, width, bricks, scale),
        out_shape=(brick_shape, brick_shape, gw_shape),
        in_specs=[hbm] * 6,
        out_specs=(hbm,) * 3,
        scratch_shapes=[
            pltpu.SMEM((bricks, VOX // 32), jnp.int32),
            pltpu.SMEM((bricks, 26), jnp.int32),
            pltpu.SMEM((1, 8), jnp.int32),
            pltpu.VMEM((width, bricks, VOX), bf16),
            pltpu.VMEM((rows_w, total), bf16),
            pltpu.VMEM((width, bricks, VOX), bf16),
            pltpu.VMEM((width, bricks, VOX), bf16),
            pltpu.VMEM((width, bricks, VOX), bf16),
            pltpu.VMEM((owners * chunk, total), bf16),
            dma((6,)), dma((3,)),
            pltpu.VMEM((bricks + 9, TILES, width, LANES), bf16),
            pltpu.VMEM((8, TILES, width, LANES), bf16),
            pltpu.VMEM((9 * LANES, 2 * LANES), bf16),
            pltpu.VMEM((LANES, 2 * LANES), bf16),
            pltpu.VMEM((2 * LANES, 9 * LANES), bf16),
            pltpu.VMEM((2 * LANES, LANES), bf16),
            pltpu.VMEM((width, bricks * cube), bf16),
            pltpu.VMEM((total, rows_k), bf16),
            pltpu.VMEM((9 * width, 3 * total), bf16),
            pltpu.VMEM((width, bricks * cube), f32),
            pltpu.VMEM((rows_k, bricks * wide), bf16),
            pltpu.VMEM((2, 2, width, bricks * VOX), bf16),
            pltpu.VMEM((2, width, bricks * VOX), bf16),
            pltpu.VMEM((2, width, bricks * VOX), bf16),
            pltpu.VMEM((2, width, bricks * VOX), bf16),
            pltpu.VMEM((2, width, bricks * VOX), bf16),
            pltpu.VMEM((2, 2, width, bricks * VOX), bf16),
            pltpu.VMEM((3 * total, bricks * cube), bf16),
            pltpu.VMEM((9 * width, bricks * cube), f32),
            pltpu.VMEM((8, TILES, width, LANES), bf16),
            pltpu.VMEM((8, TILES, width, LANES), bf16),
            pltpu.VMEM((owners * chunk, total), f32),
            pltpu.VMEM((owners * chunk, total), bf16),
            pltpu.VMEM((groups, chunk, total), bf16),
            dma((8,)), dma((8,)), dma((8,)), dma((8,)),
            dma((bricks,)), dma((bricks,)), dma((bricks,)), dma((bricks,)),
            dma((bricks,)), dma((bricks,)), dma((1,)), dma((1,)),
            dma((groups,)), dma((groups,)), dma((groups,)), dma((groups,)),
        ],
        compiler_params=pltpu.CompilerParams(
            collective_id=0, has_side_effects=True, vmem_limit_bytes=60 * 2**20
        ),
    )(
        mask_packed, neighbours, send_list.reshape(1, 8),
        features, weights.reshape(rows_w, total), cotangent,
    )
    act, grad_feat, grad_w = pl.pallas_call(
        hand_over,
        out_shape=(
            brick_shape, brick_shape, jax.ShapeDtypeStruct((rows_w, total), f32)
        ),
        in_specs=[hbm] * 3,
        out_specs=(hbm,) * 3,
        scratch_shapes=[
            pltpu.VMEM((width, bricks, VOX), bf16),
            pltpu.VMEM((width, bricks, VOX), bf16),
            pltpu.VMEM((owners * chunk, total), bf16),
            pltpu.VMEM((rows_w, total), f32),
            dma((3,)), dma((3,)),
        ],
        compiler_params=pltpu.CompilerParams(vmem_limit_bytes=60 * 2**20),
    )(*results)
    return act, grad_feat, grad_w.reshape(27, width, total)


def solution(mesh):
    return jax.shard_map(
        on_device,
        mesh=mesh,
        in_specs=(
            P("chan", "space", None),
            P("space", None),
            P("space", None),
            P("space", None, None),
            P(None, "chan", None),
            P("chan", "space", None),
        ),
        out_specs=(P("chan", "space", None), P("chan", "space", None), P(None, "chan", None)),
        check_vma=False,
    )
```

```python
import functools
import math

import jax
import jax.numpy as jnp
from jax import lax
from jax.experimental import pallas as pl
from jax.experimental.pallas import tpu as pltpu
from jax.sharding import PartitionSpec as P

BRICK = 8
VOX = 512
LANES = 128
TILES = VOX // LANES
PLANES = BRICK + 2
MESH = pl.DeviceIdType.MESH

tile_moves = [(a, b) for a in (-1, 0, 1) for b in (-1, 0, 1) if (a, b) != (0, 0)]
tile_steps = [a * 4 + b for a, b in tile_moves]
plane_offsets = [(y, z) for y in (-1, 0, 1) for z in (-1, 0, 1)]


def neighbour_slot(along_x, along_y, along_z):
    linear = (along_x + 1) * 9 + (along_y + 1) * 3 + (along_z + 1)
    return linear if linear < 13 else linear - 1


def tile_of(along_x):
    return TILES - 1 if along_x == -1 else 0


def plan_chunks(rows, groups):
    chunk = -(-rows // groups)
    chunk = -(-chunk // 16) * 16
    return chunk, -(-rows // chunk)


def nt_dot(left, right):
    return lax.dot_general(
        left, right, (((1,), (1,)), ((), ())), preferred_element_type=jnp.float32
    )


def nn_dot(left, right):
    return jnp.dot(left, right, preferred_element_type=jnp.float32)


def kernel(
    groups, parts, width, bricks, scale,
    packed_in, near_in, sends_in, feat_in, w_in, cot_in,
    act_out, grad_feat_out, gw_out,
    packed, near, sends, feat, w, cot, act, grad_feat, gw_all, in_s, out_s,
    table, outbox, place, expand, fold, compact, rimmed, w_turned, w_wide, padded, stacked, comp, mate_in, halves, cross_in, cots, gates,
    window, prod, backbox, back_in, gw_own, gw_send, gw_in,
    halo_s, halo_r, back_s, back_r, mate_s, mate_r, cross_s, cross_r, gate_s, gate_r, cot_s, cot_r, red_s, red_r, all_s, all_r,
):
    me, mine = lax.axis_index("space"), lax.axis_index("chan")
    total = parts * width
    rows_w = 27 * width
    chunk, owners = plan_chunks(rows_w, groups)
    wide = BRICK * LANES
    cube = PLANES * LANES
    f32, bf16 = jnp.float32, jnp.bfloat16

    fetches = [
        pltpu.make_async_copy(source, target, in_s.at[i])
        for i, (source, target) in enumerate(
            (
                (packed_in, packed), (feat_in, feat), (sends_in, sends), (near_in, near),
                (cot_in, cot), (w_in, w),
            )
        )
    ]
    for fetch in fetches:
        fetch.start()
    level, low = mine // 2, lax.rem(mine, 2)
    mate, across = mine + 1 - 2 * low, lax.rem(mine + 2, 4)

    barrier = pltpu.get_barrier_semaphore()
    for d in range(1, groups):
        pl.semaphore_signal(
            barrier, inc=1, device_id=(lax.rem(me + d, groups), mine), device_id_type=MESH
        )
    for peer in (mate, across):
        pl.semaphore_signal(barrier, inc=1, device_id=(me, peer), device_id_type=MESH)

    row = lax.broadcasted_iota(jnp.int32, (LANES, 2 * LANES), 0)
    col = lax.broadcasted_iota(jnp.int32, (LANES, 2 * LANES), 1)
    half, at_y, at_z = row >> 6, (row >> 3) & 7, row & 7
    goal = half * LANES + (at_y + 1) * PLANES + (at_z + 1)
    side_y = {-1: at_y == BRICK - 1, 1: at_y == 0}
    side_z = {-1: at_z == BRICK - 1, 1: at_z == 0}
    for n, (y, z) in enumerate(plane_offsets):
        hit = col == goal + (BRICK * PLANES * y + BRICK * z)
        if y != 0:
            hit = hit & side_y[y]
        if z != 0:
            hit = hit & side_z[z]
        place[n * LANES : (n + 1) * LANES, :] = jnp.where(hit, 1.0, 0.0).astype(bf16)
    row_t = lax.broadcasted_iota(jnp.int32, (2 * LANES, LANES), 0)
    col_t = lax.broadcasted_iota(jnp.int32, (2 * LANES, LANES), 1)
    goal_t = (col_t >> 6) * LANES + (((col_t >> 3) & 7) + 1) * PLANES + ((col_t & 7) + 1)
    compact[...] = jnp.where(row_t == goal_t - (PLANES + 1), 1.0, 0.0).astype(bf16)
    expand[...] = jnp.where(col == goal - (PLANES + 1), 1.0, 0.0).astype(bf16)

    for fetch in fetches[:3]:
        fetch.wait()

    lane = lax.broadcasted_iota(jnp.int32, (1, VOX), 1)
    masks = []
    for b in range(bricks):
        word = jnp.zeros((1, VOX), jnp.int32)
        for i in range(VOX // 32):
            word = jnp.where((lane >> 5) == i, packed[b, i], word)
        masks.append((lax.shift_right_logical(word, lane & 31) & 1).astype(f32))

    masked = [
        feat[:, b, :].astype(f32) * masks[b] for b in range(bricks)
    ]
    for b in range(bricks):
        for t in range(TILES):
            table[b, t] = masked[b][:, t * LANES : (t + 1) * LANES].astype(bf16)
    table[bricks + 8] = jnp.zeros((TILES, width, LANES), bf16)
    for k, (a, _) in enumerate(tile_moves):
        chosen = jnp.full((width, LANES), sends[0, k], jnp.int32)
        for t in range(TILES) if a == 0 else (tile_of(a),):
            value = jnp.zeros((width, LANES), f32)
            for b in range(bricks):
                value = jnp.where(chosen == b, masked[b][:, t * LANES : (t + 1) * LANES], value)
            outbox[k, t] = value.astype(bf16)

    pl.semaphore_wait(barrier, groups - 1 + 2)

    tile_a, tile_b = me // 4, lax.rem(me, 4)

    def inside(a, b):
        return (
            (tile_a + a >= 0) & (tile_a + a < groups // 4) & (tile_b + b >= 0) & (tile_b + b < 4)
        )

    def halo(k, box, rows, base, send, recv, sign):
        a, _ = tile_moves[k]
        if a == 0:
            source, target = box.at[k], rows.at[base + k]
        else:
            source, target = box.at[k, tile_of(a)], rows.at[base + k, tile_of(a)]
        peer = jnp.clip(me + sign * tile_steps[k], 0, groups - 1)
        return pltpu.make_async_remote_copy(
            src_ref=source, dst_ref=target, send_sem=send.at[k], recv_sem=recv.at[k],
            device_id=(peer, mine), device_id_type=MESH,
        )

    forth = [halo(k, outbox, table, bricks, halo_s, halo_r, -1) for k in range(8)]
    back = [halo(k, backbox, back_in, 0, back_s, back_r, 1) for k in range(8)]
    ahead = [inside(a, b) for a, b in tile_moves]
    behind = [inside(-a, -b) for a, b in tile_moves]

    def start_if(flag, copy):
        @pl.when(flag)
        def _():
            copy.start()

    def sent_if(flag, copy):
        @pl.when(flag)
        def _():
            copy.wait_send()

    def arrived_if(flag, copy):
        @pl.when(flag)
        def _():
            copy.wait_recv()

    for k in range(8):
        start_if(behind[k], forth[k])

    for fetch in fetches[3:]:
        fetch.wait()
    for b in range(bricks):
        cots[level, :, b * VOX : (b + 1) * VOX] = cot[:, b, :]
    cot_copy = pltpu.make_async_remote_copy(
        src_ref=cots.at[level], dst_ref=cots.at[level], send_sem=cot_s.at[0],
        recv_sem=cot_r.at[0], device_id=(me, across), device_id_type=MESH,
    )
    cot_copy.start()

    rows_k = w_turned.shape[1]
    for c in range(rows_k // LANES):
        have = min(rows_w - c * LANES, LANES)
        block = w[c * LANES : c * LANES + have, :].astype(f32)
        if have < LANES:
            block = jnp.concatenate([block, jnp.zeros((LANES - have, total), f32)], axis=0)
        w_turned[:, c * LANES : (c + 1) * LANES] = block.T.astype(bf16)
    if rows_k > rows_w:
        stacked[rows_w:, :] = jnp.zeros((rows_k - rows_w, bricks * wide), bf16)
    for k in range(8):
        arrived_if(ahead[k], forth[k])

    columns = []
    for n, (y, z) in enumerate(plane_offsets):
        pieces = []
        for b in range(bricks):
            source = b if (y, z) == (0, 0) else near[b, neighbour_slot(0, y, z)]
            pieces.append(table[source].reshape(TILES * width, LANES))
        for x in (-1, 1):
            for b in range(bricks):
                pieces.append(table[near[b, neighbour_slot(x, y, z)], tile_of(x)])
        columns.append(jnp.concatenate(pieces, axis=0))
    built = nn_dot(jnp.concatenate(columns, axis=1), place[...]).astype(bf16)
    ends = bricks * TILES * width
    for b in range(bricks):
        base = b * cube
        first = ends + b * width
        last = ends + (bricks + b) * width
        rimmed[:, base : base + LANES] = built[first : first + width, LANES:]
        rimmed[:, base + cube - LANES : base + cube] = built[last : last + width, :LANES]
        for t in range(TILES):
            at = (b * TILES + t) * width
            rimmed[:, base + (2 * t + 1) * LANES : base + (2 * t + 3) * LANES] = built[
                at : at + width, :
            ]

    length = bricks * cube
    shifts = [(y + 1) * PLANES + (z + 1) for y, z in plane_offsets]
    for n in range(9):
        value = rimmed[...]
        if shifts[n]:
            value = pltpu.roll(value, length - shifts[n], axis=1)
        for u in range(3):
            for b in range(bricks):
                stacked[
                    (u * 9 + n) * width : (u * 9 + n + 1) * width, b * wide : (b + 1) * wide
                ] = value[:, b * cube + u * LANES : b * cube + u * LANES + wide]

    def chan_copy(source, target, send, recv, peer):
        return pltpu.make_async_remote_copy(
            src_ref=source, dst_ref=target, send_sem=send, recv_sem=recv,
            device_id=(me, peer), device_id_type=MESH,
        )

    spans = [pl.ds(b * VOX, VOX) for b in range(bricks)]
    to_mate = [
        chan_copy(
            comp.at[:, 1 - low, :, spans[b]], mate_in.at[:, :, spans[b]],
            mate_s.at[b], mate_r.at[b], mate,
        )
        for b in range(bricks)
    ]
    to_across = [
        chan_copy(
            halves.at[:, :, spans[b]], cross_in.at[:, :, spans[b]],
            cross_s.at[b], cross_r.at[b], across,
        )
        for b in range(bricks)
    ]
    to_both = [
        chan_copy(
            gates.at[:, low, :, spans[b]], gates.at[:, low, :, spans[b]],
            gate_s.at[b], gate_r.at[b], mate,
        )
        for b in range(bricks)
    ]

    for b in range(bricks):
        for t in range(TILES):
            i = b * TILES + t
            part = nn_dot(w_turned[...], stacked[:, 2 * i * LANES : 2 * (i + 1) * LANES])
            comp[:, :, :, i * LANES : (i + 1) * LANES] = (
                nn_dot(part.astype(bf16), compact[...])
                .astype(bf16)
                .reshape(2, 2, width, LANES)
            )
        to_mate[b].start()

    for b in range(bricks):
        to_mate[b].wait_recv()
        halves[:, :, spans[b]] = (
            comp[:, low, :, spans[b]].astype(f32) + mate_in[:, :, spans[b]].astype(f32)
        ).astype(bf16)
        to_across[b].start()

    for n in range(9):
        for u in range(3):
            w_wide[n * width : (n + 1) * width, u * total : (u + 1) * total] = w[
                (u * 9 + n) * width : (u * 9 + n + 1) * width, :
            ]
    for u in range(3):
        for b in range(bricks):
            for px in range(PLANES):
                if not u <= px < u + BRICK:
                    window[
                        u * total : (u + 1) * total,
                        b * cube + px * LANES : b * cube + (px + 1) * LANES,
                    ] = jnp.zeros((total, LANES), bf16)

    for n, (y, z) in enumerate(plane_offsets):
        hit = row_t == goal_t + (BRICK * PLANES * y + BRICK * z)
        if y != 0:
            hit = hit & ((col_t >> 3) & 7 == (BRICK - 1 if y == -1 else 0))
        if z != 0:
            hit = hit & (col_t & 7 == (BRICK - 1 if z == -1 else 0))
        fold[:, n * LANES : (n + 1) * LANES] = jnp.where(hit, 1.0, 0.0).astype(bf16)

    cot_copy.wait_recv()
    for b in range(bricks):
        to_across[b].wait_recv()
        for h in range(2):
            pre = halves[h, :, spans[b]].astype(f32) + cross_in[h, :, spans[b]].astype(f32)
            pre = pre * masks[b]
            gate = jax.nn.sigmoid(pre)
            gates[h, low, :, spans[b]] = (
                cots[h, :, spans[b]].astype(f32) * masks[b] * gate * (1.0 + pre * (1.0 - gate))
            ).astype(bf16)

        to_both[b].start()
    for b in range(bricks):
        pre = halves[level, :, spans[b]].astype(f32) + cross_in[level, :, spans[b]].astype(f32)
        pre = pre * masks[b]
        act[:, b, :] = (pre * jax.nn.sigmoid(pre)).astype(bf16)
    act_copy = pltpu.make_async_copy(act, act_out, out_s.at[0])
    act_copy.start()

    for b in range(bricks):
        to_both[b].wait_recv()
        for t in range(TILES):
            i = b * TILES + t
            value = gates[:, :, :, i * LANES : (i + 1) * LANES].reshape(total, LANES)
            value = nn_dot(value, expand[...]).astype(bf16)
            for u in range(3):
                at = b * cube + (u + 2 * t) * LANES
                window[u * total : (u + 1) * total, at : at + 2 * LANES] = value

    def chunk_rows(index):
        return pl.ds(pl.multiple_of(index * chunk, 16), chunk)

    def reduce_copy(d):
        peer = lax.rem(me + d, groups)
        kept = jnp.minimum(peer, owners - 1)
        return peer, pltpu.make_async_remote_copy(
            src_ref=gw_send.at[chunk_rows(kept)], dst_ref=gw_in.at[d],
            send_sem=red_s.at[d], recv_sem=red_r.at[d],
            device_id=(peer, mine), device_id_type=MESH,
        )

    kept_me = jnp.minimum(me, owners - 1)

    def share_copy(d):
        peer = lax.rem(me + d, groups)
        span = gw_all.at[chunk_rows(kept_me)]
        return pltpu.make_async_remote_copy(
            src_ref=span, dst_ref=span, send_sem=all_s.at[d], recv_sem=all_r.at[d],
            device_id=(peer, mine), device_id_type=MESH,
        )

    def guarded(flag, action):
        if owners == groups:
            action()
        else:
            pl.when(flag)(action)

    pack = 2 if owners % 2 == 0 else 1
    packs = owners // pack
    for i in range(packs):
        first = lax.rem(me // pack + i + 1, packs) * pack
        span = pl.ds(pl.multiple_of(first * chunk, 16), pack * chunk)
        value = None
        for b in range(bricks):
            term = nt_dot(
                stacked[span, b * wide : (b + 1) * wide],
                window[total : 2 * total, b * cube + LANES : b * cube + LANES + wide],
            )
            value = term if value is None else value + term
        gw_own[span, :] = value
        gw_send[span, :] = value.astype(bf16)
        for c in range(pack):
            copy = reduce_copy(lax.rem(first + c - me + groups, groups))[1]
            if groups == owners and i < packs - 1:
                copy.start()
            else:
                pl.when(first + c != me)(copy.start)

    for i in range(length // (2 * LANES)):
        span = slice(2 * i * LANES, 2 * (i + 1) * LANES)
        prod[:, span] = nn_dot(w_wide[...], window[:, span])
    spread = prod[0:width, :]
    for n in range(1, 9):
        spread = spread + pltpu.roll(prod[n * width : (n + 1) * width, :], shifts[n], axis=1)
    padded[...] = spread

    def add_up():
        value = gw_own[chunk_rows(kept_me), :]
        for d in range(1, groups):
            reduce_copy(d)[1].wait_recv()
            value = value + gw_in[d].astype(f32)
        gw_all[chunk_rows(kept_me), :] = (value * scale).astype(bf16)
        for d in range(1, groups):
            share_copy(d).start()

    guarded(me < owners, add_up)

    pieces = []
    blank = jnp.zeros((width, LANES), f32)
    for b in range(bricks):
        for t in range(TILES):
            at = b * cube + (2 * t + 1) * LANES
            pieces.append(padded[:, at : at + 2 * LANES])
    for b in range(bricks):
        pieces.append(jnp.concatenate([blank, padded[:, b * cube : b * cube + LANES]], axis=1))
    for b in range(bricks):
        at = (b + 1) * cube - LANES
        pieces.append(jnp.concatenate([padded[:, at : at + LANES], blank], axis=1))
    rims = jnp.concatenate(pieces, axis=0).astype(bf16)

    whole = TILES * width
    own = [jnp.zeros((whole, LANES), f32) for _ in range(bricks)]
    own_end = {(b, x): blank for b in range(bricks) for x in (-1, 1)}
    slots = [jnp.zeros((whole if a == 0 else width, LANES), f32) for a, _ in tile_moves]

    def weighed(index, wanted, value):
        return value * jnp.where(index == wanted, 1.0, 0.0).astype(f32)

    def picked(index, wanted, value):
        return jnp.where(jnp.full(value.shape, index, jnp.int32) == wanted, value, 0.0)

    for n, (y, z) in enumerate(plane_offsets):
        folded = nn_dot(rims, fold[:, n * LANES : (n + 1) * LANES])
        for x in (-1, 0, 1):
            slot = None if (x, y) == (0, 0) else tile_moves.index((x, y))
            for b in range(bricks):
                if x == 0:
                    piece = folded[b * whole : (b + 1) * whole]
                else:
                    at = ends + (b if x == -1 else bricks + b) * width
                    piece = folded[at : at + width]
                if (x, y, z) == (0, 0, 0):
                    own[b] = own[b] + piece
                    continue
                index = near[b, neighbour_slot(x, y, z)]
                for c in range(bricks):
                    term = weighed(index, c, piece)
                    if x == 0:
                        own[c] = own[c] + term
                    else:
                        own_end[c, x] = own_end[c, x] + term
                if slot is not None:
                    slots[slot] = slots[slot] + weighed(index, bricks + slot, piece)
    for k, (a, _) in enumerate(tile_moves):
        if a == 0:
            backbox[k] = slots[k].astype(bf16).reshape(TILES, width, LANES)
        else:
            backbox[k, tile_of(a)] = slots[k].astype(bf16)
        start_if(ahead[k], back[k])

    for k in range(8):
        arrived_if(behind[k], back[k])
    for b in range(bricks):
        rows = []
        for t in range(TILES):
            value = own[b][t * width : (t + 1) * width]
            for x in (-1, 1):
                if t == tile_of(x):
                    value = value + own_end[b, x]
            for k, (a, _) in enumerate(tile_moves):
                if a == 0 or t == tile_of(a):
                    value = value + picked(sends[0, k], b, back_in[k, t].astype(f32))
            rows.append((value * masks[b][:, t * LANES : (t + 1) * LANES]).astype(bf16))
        grad_feat[:, b, :] = jnp.concatenate(rows, axis=1)
    feat_copy = pltpu.make_async_copy(grad_feat, grad_feat_out, out_s.at[1])
    feat_copy.start()

    for d in range(1, groups):
        source = lax.rem(me + groups - d, groups)
        guarded(source < owners, share_copy(d).wait_recv)
    gw_copy = pltpu.make_async_copy(gw_all, gw_out, out_s.at[2])
    gw_copy.start()

    for k in range(8):
        sent_if(behind[k], forth[k])
        sent_if(ahead[k], back[k])
    for b in range(bricks):
        to_mate[b].wait_send()
        to_across[b].wait_send()
        to_both[b].wait_send()
    cot_copy.wait_send()
    for d in range(1, groups):
        peer, copy = reduce_copy(d)
        guarded(peer < owners, copy.wait_send)
        guarded(me < owners, share_copy(d).wait_send)
    act_copy.wait()
    feat_copy.wait()
    gw_copy.wait()


def hand_over(*refs):
    sources, targets, held, wide, in_s, out_s = refs[:3], refs[3:6], refs[6:9], refs[9], *refs[10:]
    fetches = [pltpu.make_async_copy(sources[i], held[i], in_s.at[i]) for i in range(3)]
    stores = [
        pltpu.make_async_copy(source, targets[i], out_s.at[i])
        for i, source in enumerate((held[0], held[1], wide))
    ]
    for fetch in fetches:
        fetch.start()
    for i in range(3):
        fetches[i].wait()
        if i == 2:
            wide[...] = held[2][0 : wide.shape[0], :].astype(jnp.float32)
        stores[i].start()
    for store in stores:
        store.wait()


def on_device(features, mask_packed, neighbours, send_list, weights, cotangent):
    groups, parts = lax.axis_size("space"), lax.axis_size("chan")
    width, bricks = features.shape[0], features.shape[1]
    total = weights.shape[2]
    rows_w = 27 * width
    chunk, owners = plan_chunks(rows_w, groups)
    rows_k = -(-max(rows_w, owners * chunk) // LANES) * LANES
    wide, cube = BRICK * LANES, PLANES * LANES
    scale = 1.0 / math.sqrt(bricks * groups * VOX)
    f32, bf16 = jnp.float32, jnp.bfloat16
    dma = pltpu.SemaphoreType.DMA
    brick_shape = jax.ShapeDtypeStruct((width, bricks, VOX), bf16)
    gw_shape = jax.ShapeDtypeStruct((owners * chunk, total), bf16)
    hbm = pl.BlockSpec(memory_space=pl.ANY)
    results = pl.pallas_call(
        functools.partial(kernel, groups, parts, width, bricks, scale),
        out_shape=(brick_shape, brick_shape, gw_shape),
        in_specs=[hbm] * 6,
        out_specs=(hbm,) * 3,
        scratch_shapes=[
            pltpu.SMEM((bricks, VOX // 32), jnp.int32),
            pltpu.SMEM((bricks, 26), jnp.int32),
            pltpu.SMEM((1, 8), jnp.int32),
            pltpu.VMEM((width, bricks, VOX), bf16),
            pltpu.VMEM((rows_w, total), bf16),
            pltpu.VMEM((width, bricks, VOX), bf16),
            pltpu.VMEM((width, bricks, VOX), bf16),
            pltpu.VMEM((width, bricks, VOX), bf16),
            pltpu.VMEM((owners * chunk, total), bf16),
            dma((6,)), dma((3,)),
            pltpu.VMEM((bricks + 9, TILES, width, LANES), bf16),
            pltpu.VMEM((8, TILES, width, LANES), bf16),
            pltpu.VMEM((9 * LANES, 2 * LANES), bf16),
            pltpu.VMEM((LANES, 2 * LANES), bf16),
            pltpu.VMEM((2 * LANES, 9 * LANES), bf16),
            pltpu.VMEM((2 * LANES, LANES), bf16),
            pltpu.VMEM((width, bricks * cube), bf16),
            pltpu.VMEM((total, rows_k), bf16),
            pltpu.VMEM((9 * width, 3 * total), bf16),
            pltpu.VMEM((width, bricks * cube), f32),
            pltpu.VMEM((rows_k, bricks * wide), bf16),
            pltpu.VMEM((2, 2, width, bricks * VOX), bf16),
            pltpu.VMEM((2, width, bricks * VOX), bf16),
            pltpu.VMEM((2, width, bricks * VOX), bf16),
            pltpu.VMEM((2, width, bricks * VOX), bf16),
            pltpu.VMEM((2, width, bricks * VOX), bf16),
            pltpu.VMEM((2, 2, width, bricks * VOX), bf16),
            pltpu.VMEM((3 * total, bricks * cube), bf16),
            pltpu.VMEM((9 * width, bricks * cube), f32),
            pltpu.VMEM((8, TILES, width, LANES), bf16),
            pltpu.VMEM((8, TILES, width, LANES), bf16),
            pltpu.VMEM((owners * chunk, total), f32),
            pltpu.VMEM((owners * chunk, total), bf16),
            pltpu.VMEM((groups, chunk, total), bf16),
            dma((8,)), dma((8,)), dma((8,)), dma((8,)),
            dma((bricks,)), dma((bricks,)), dma((bricks,)), dma((bricks,)),
            dma((bricks,)), dma((bricks,)), dma((1,)), dma((1,)),
            dma((groups,)), dma((groups,)), dma((groups,)), dma((groups,)),
        ],
        compiler_params=pltpu.CompilerParams(
            collective_id=0, has_side_effects=True, vmem_limit_bytes=60 * 2**20
        ),
    )(
        mask_packed, neighbours, send_list.reshape(1, 8),
        features, weights.reshape(rows_w, total), cotangent,
    )
    act, grad_feat, grad_w = pl.pallas_call(
        hand_over,
        out_shape=(
            brick_shape, brick_shape, jax.ShapeDtypeStruct((rows_w, total), f32)
        ),
        in_specs=[hbm] * 3,
        out_specs=(hbm,) * 3,
        scratch_shapes=[
            pltpu.VMEM((width, bricks, VOX), bf16),
            pltpu.VMEM((width, bricks, VOX), bf16),
            pltpu.VMEM((owners * chunk, total), bf16),
            pltpu.VMEM((rows_w, total), f32),
            dma((3,)), dma((3,)),
        ],
        compiler_params=pltpu.CompilerParams(vmem_limit_bytes=60 * 2**20),
    )(*results)
    return act, grad_feat, grad_w.reshape(27, width, total)


def solution(mesh):
    return jax.shard_map(
        on_device,
        mesh=mesh,
        in_specs=(
            P("chan", "space", None),
            P("space", None),
            P("space", None),
            P("space", None, None),
            P(None, "chan", None),
            P("chan", "space", None),
        ),
        out_specs=(P("chan", "space", None), P("chan", "space", None), P(None, "chan", None)),
        check_vma=False,
    )
```
